256 devices in a mesh: dom: 4 (over y_lo, core), dev: 64 (over x, y_hi, z).
Axes of the slice: x: 4, y: 4 (y_hi: 2, y_lo: 2; y = y_hi * 2 + y_lo), z: 8, core: 2. Of those that a mesh axis runs over, the one named last changes fastest.
Arguments:
- features: bfloat16 [262144, 256], P(('dom', 'dev')), may hold values from -6 to 6
- weight: bfloat16 [256, 256], replicated, may hold values from -0.375 to 0.375
- cotangent: bfloat16 [262144, 256], P(('dom', 'dev')), may hold values from -6 to 6
- send_list: int32 [4, 64, 64, 1], P('dom', 'dev'), may hold values from 0 to 7
- intra_rows: int32 [4, 64, 32], P('dom', 'dev'), may hold values from 0 to 7
- intra_src: int32 [4, 64, 32], P('dom', 'dev'), may hold values from 0 to 63
- intra_count: int32 [4, 64], P('dom', 'dev'), may hold values from 8 to 32, as said below
- intra_vals: bfloat16 [4, 64, 32, 128, 128], P('dom', 'dev'), may hold values from -0.15625 to 0.15625
- cross_rows: int32 [4, 64, 3, 16], P('dom', 'dev'), may hold values from 0 to 7
- cross_cols: int32 [4, 64, 3, 16], P('dom', 'dev'), may hold values from 0 to 7
- cross_vals: bfloat16 [4, 64, 3, 16, 128, 128], P('dom', 'dev'), may hold values from -0.15625 to 0.15625
Outputs:
- activated: bfloat16 [262144, 256], P(('dom', 'dev'))
- input_grad: bfloat16 [262144, 256], P(('dom', 'dev'))
- weight_grad: float32 [256, 256], replicated
The draws below stay inside these ranges and needn't reach their ends.
Inputs may be any that keep to these rules, and one draw needn't show every extreme that they name: `intra_count`: each device has from 8 to 32 live tiles inside its partition; some device has exactly 32.
All inputs are finite; a program needn't handle non-finite values.
Results may differ from the reference program's by a relative error of at most 0.0061.
Values may be sent and summed in bfloat16 or wider, within the bound.
A program may use at most 128 MiB of HBM per device.

```python
import math
import jax
import jax.numpy as jnp
from jax import lax

F = 256
BLK = 128
CAP = 1
RB = 8
KIN = 32
KX = 16
NODES = 262144
N_DOM = 4
N_DEV = 64


def draw_intra_count(key, part):
    counts = jax.random.randint(key, (N_DOM * N_DEV,), KIN // 4, KIN + 1)
    chosen = jax.random.randint(jax.random.fold_in(key, 7), (), 0, N_DOM * N_DEV)
    counts = jnp.where(jnp.arange(N_DOM * N_DEV) == chosen, KIN, counts)
    return counts.reshape(N_DOM, N_DEV).astype(jnp.int32)


def touch_ends(result, own_key, low, largest):
    longest = result.shape.index(max(result.shape))
    spots = []
    for shift in (0, 1):
        where = [jax.random.randint(jax.random.fold_in(own_key, axis), (), 0, length) for axis, length in enumerate(result.shape)]
        where[longest] = (where[longest] + shift) % result.shape[longest]
        spots.append(tuple(where))
    return result.at[spots[0]].set(low).at[spots[1]].set(largest)


def levels(own_key, dims, split, smallest, high):
    gain = 1.0
    for dim, shards_of in split:
        draws = jax.random.uniform(jax.random.fold_in(jax.random.fold_in(own_key, 6), dim), (shards_of,), jnp.float32, smallest / len(split), high / len(split))
        gain = gain * jnp.repeat(jnp.exp(draws), dims[dim] // shards_of).reshape((-1,) + (1,) * (len(dims) - 1 - dim))
    return gain


def bell_draw(own_key, shape, spread, reach, shards=(), held_as=jnp.bfloat16):
    result = spread * jax.random.normal(own_key, shape, jnp.float32)
    if shards:
        result = result * levels(own_key, shape, shards, -0.22, 0.18)
    return jnp.clip(result, -reach, reach).astype(held_as)


def setup_inputs(seed: int = 0) -> dict:
    streams_of = jax.random.split(jax.random.key(seed), 12)
    features = bell_draw(streams_of[0], (NODES, F), 1.0, 6.0, ((0, 256),))
    weight = bell_draw(streams_of[1], (F, F), F ** -0.5, 0.375)
    cotangent = bell_draw(streams_of[2], (NODES, F), 1.0, 6.0, ((0, 256),))
    send_list = touch_ends(jax.random.randint(streams_of[3], (N_DOM, N_DEV, N_DEV, CAP), 0, RB), jax.random.fold_in(streams_of[3], 1), 0, RB - 1).astype(jnp.int32)
    intra_rows = touch_ends(jax.random.randint(streams_of[4], (N_DOM, N_DEV, KIN), 0, RB), jax.random.fold_in(streams_of[4], 1), 0, RB - 1).astype(jnp.int32)
    intra_src = touch_ends(jax.random.randint(streams_of[5], (N_DOM, N_DEV, KIN), 0, N_DEV * CAP), jax.random.fold_in(streams_of[5], 1), 0, (N_DEV * CAP) - 1).astype(jnp.int32)
    intra_count = draw_intra_count(jax.random.fold_in(streams_of[11], 71), 0)
    intra_vals = bell_draw(streams_of[7], (N_DOM, N_DEV, KIN, BLK, BLK), (BLK * (KIN + (N_DOM - 1) * KX) // RB) ** -0.5, 0.15625, ((0, 4), (1, 64)))
    cross_rows = touch_ends(jax.random.randint(streams_of[8], (N_DOM, N_DEV, N_DOM - 1, KX), 0, RB), jax.random.fold_in(streams_of[8], 1), 0, RB - 1).astype(jnp.int32)
    cross_cols = touch_ends(jax.random.randint(streams_of[9], (N_DOM, N_DEV, N_DOM - 1, KX), 0, RB), jax.random.fold_in(streams_of[9], 1), 0, RB - 1).astype(jnp.int32)
    cross_vals = bell_draw(streams_of[10], (N_DOM, N_DEV, N_DOM - 1, KX, BLK, BLK), (BLK * (KIN + (N_DOM - 1) * KX) // RB) ** -0.5, 0.15625, ((0, 4), (1, 64)))
    return {"features": features, "weight": weight, "cotangent": cotangent, "send_list": send_list, "intra_rows": intra_rows, "intra_src": intra_src, "intra_count": intra_count, "intra_vals": intra_vals, "cross_rows": cross_rows, "cross_cols": cross_cols, "cross_vals": cross_vals}


def aggregate(feat_f32, send_list, intra_rows, intra_src, live_mask, intra_vals, cross_rows, cross_cols, cross_vals):

    def per_device(device):
        dom_at = device // N_DEV
        dev_at = device % N_DEV
        source = intra_src[dom_at, dev_at]
        peer_dev = source // CAP
        slot_at = source % CAP
        blocks = send_list[dom_at, peer_dev, dev_at, slot_at]
        picked = feat_f32[dom_at, peer_dev, blocks]
        tile_vals = intra_vals[dom_at, dev_at].astype(jnp.float32) * live_mask[dom_at, dev_at][:, None, None]
        contrib = jnp.einsum('kab,kbf->kaf', tile_vals, picked, precision=lax.Precision.HIGHEST)
        summed = jnp.zeros((RB, BLK, F), jnp.float32).at[intra_rows[dom_at, dev_at]].add(contrib)
        anchor = (dom_at - 1 - jnp.arange(N_DOM - 1)) % N_DOM
        cross_in = feat_f32[anchor[:, None], dev_at, cross_cols[dom_at, dev_at]]
        cross_out = jnp.einsum('okab,okbf->okaf', cross_vals[dom_at, dev_at].astype(jnp.float32), cross_in, precision=lax.Precision.HIGHEST)
        return summed.at[cross_rows[dom_at, dev_at]].add(cross_out)
    return lax.map(per_device, jnp.arange(N_DOM * N_DEV))

def transpose_aggregate(back_f32, send_list, intra_rows, intra_src, live_mask, intra_vals, cross_rows, cross_cols, cross_vals):

    def add_device(device, summed):
        dom_at = device // N_DEV
        dev_at = device % N_DEV
        source = intra_src[dom_at, dev_at]
        peer_dev = source // CAP
        slot_at = source % CAP
        blocks = send_list[dom_at, peer_dev, dev_at, slot_at]
        back_blocks = back_f32[dom_at, dev_at]
        tile_vals = intra_vals[dom_at, dev_at].astype(jnp.float32) * live_mask[dom_at, dev_at][:, None, None]
        contrib = jnp.einsum('kab,kaf->kbf', tile_vals, back_blocks[intra_rows[dom_at, dev_at]], precision=lax.Precision.HIGHEST)
        summed = summed.at[dom_at, peer_dev, blocks].add(contrib)
        anchor = (dom_at - 1 - jnp.arange(N_DOM - 1)) % N_DOM
        cross_out = jnp.einsum('okab,okaf->okbf', cross_vals[dom_at, dev_at].astype(jnp.float32), back_blocks[cross_rows[dom_at, dev_at]], precision=lax.Precision.HIGHEST)
        return summed.at[anchor[:, None], dev_at, cross_cols[dom_at, dev_at]].add(cross_out)
    start = jnp.zeros((N_DOM, N_DEV, RB, BLK, F), jnp.float32)
    return lax.fori_loop(0, N_DOM * N_DEV, add_device, start)

def reference(features, weight, cotangent, send_list, intra_rows, intra_src, intra_count, intra_vals, cross_rows, cross_cols, cross_vals):
    live_mask = (jnp.arange(KIN)[None, None, :] < intra_count[:, :, None]).astype(jnp.float32)
    tables = (send_list, intra_rows, intra_src, live_mask, intra_vals, cross_rows, cross_cols, cross_vals)
    feat_f32 = features.astype(jnp.float32).reshape(N_DOM, N_DEV, RB, BLK, F)
    aggregated = aggregate(feat_f32, *tables).reshape(NODES, F).astype(jnp.bfloat16)
    pre_act = jnp.dot(aggregated, weight, preferred_element_type=jnp.float32)
    activated = jax.nn.silu(pre_act).astype(jnp.bfloat16)
    sigmoid_v = jax.nn.sigmoid(pre_act)
    pre_grad = (cotangent.astype(jnp.float32) * sigmoid_v * (1.0 + pre_act * (1.0 - sigmoid_v))).astype(jnp.bfloat16)
    weight_grad = jnp.dot(aggregated.T, pre_grad, preferred_element_type=jnp.float32) / math.sqrt(NODES)
    back_grad = jnp.dot(pre_grad, weight.T, preferred_element_type=jnp.float32).astype(jnp.bfloat16)
    back_f32 = back_grad.astype(jnp.float32).reshape(N_DOM, N_DEV, RB, BLK, F)
    input_grad = transpose_aggregate(back_f32, *tables).reshape(NODES, F).astype(jnp.bfloat16)
    return (activated, input_grad, weight_grad)
```

```python
import functools
import math

import jax
import jax.numpy as jnp
from jax import lax
from jax.experimental import pallas as pl
from jax.experimental.pallas import tpu as pltpu
from jax.sharding import PartitionSpec as P

MESH = pl.DeviceIdType.MESH
BF = jnp.bfloat16
F32 = jnp.float32
NX, NY, NZ = 4, 2, 8
RB, BLK, F = 8, 128, 256
N_DOM = 4
KIN, KX = 32, 16
HALF = RB // 2
RELS = (0, -1, 1, -2, 2, -3, 3, 4)
SLOT = {rel: i for i, rel in enumerate(RELS)}


def position():
    dom = lax.axis_index("dom")
    dev = lax.axis_index("dev")
    return dom, dev, dev // 16, (dev // 8) % 2, dev % 8


def dev_of(x, yh, z):
    return x * 16 + yh * 8 + z


def remote(src, dst, send_sem, recv_sem, dom, dev):
    return pltpu.make_async_remote_copy(
        src_ref=src, dst_ref=dst, send_sem=send_sem, recv_sem=recv_sem,
        device_id=(dom, dev), device_id_type=MESH)


def greet(peers):
    barrier = pltpu.get_barrier_semaphore()
    for dom, dev in peers:
        pl.semaphore_signal(barrier, inc=1, device_id=(dom, dev), device_id_type=MESH)
    pl.semaphore_wait(barrier, len(peers))


def gather_kernel(feat, slots_sm, slots_vm, pool, rem, tab,
                  b1, b2, b3, b4, b5, b6, b7, stage, relay, tab_vm, tab_sm,
                  meta_s, meta_r, zs, zr, xs, xr, ys, yr, ls, ds, dr, ts):
    dom, dev, x, yh, z = position()
    yo = 1 - yh
    bufs = dict(zip(RELS, (feat, b1, b2, b3, b4, b5, b6, b7)))

    def zdev(rel):
        return dev_of(x, yh, (z + rel + NZ) % NZ)

    def xdev(dx):
        return dev_of((x + dx) % NX, yh, z)

    ydev = dev_of(x, yo, z)
    sib = dom + 1 - 2 * (dom % 2)
    far = (dom + 2) % N_DOM

    greet([(dom, zdev(rel)) for rel in RELS[1:]] + [(dom, xdev(dx)) for dx in (1, 2, 3)]
          + [(dom, ydev), (sib, dev), (far, dev)])

    live = []

    def go(copy):
        copy.start()
        live.append(copy)
        return copy

    for rel in RELS[1:]:
        i = SLOT[-rel] if rel != 4 else SLOT[4]
        go(remote(slots_vm, tab_vm.at[i], meta_s.at[i], meta_r.at[i], dom, zdev(rel)))

    def zcopy(src_rel, dst_rel, piece, step):
        part = pl.ds(piece * HALF, HALF)
        s = SLOT[dst_rel] * 2 + piece
        return remote(bufs[src_rel].at[part], bufs[dst_rel].at[part], zs.at[s], zr.at[s], dom, zdev(step))

    for n in (0, 1):
        go(zcopy(0, -1, n, 1))
        go(zcopy(0, 1, 1 - n, -1))
    o_sib = (sib - dom - 1 + 2 * N_DOM) % N_DOM
    go(remote(feat, rem.at[o_sib], ds.at[0], dr.at[0], sib, dev))
    go(remote(feat, rem.at[1], ds.at[1], dr.at[1], far, dev))

    def serve(rel):
        i = SLOT[rel]
        buf = bufs[rel]
        zsrc = (z + rel + NZ) % NZ
        for xx in range(NX):
            for g, y in ((0, yo), (1, yh)):
                where = dev_of(xx, y, z)
                if rel == 0:
                    pick = slots_sm[where]
                else:
                    pick = tab_sm[i, 0, where]
                stage[i, g, xx] = buf[pick]
        go(remote(stage.at[i, 0], relay.at[i], ys.at[i], yr.at[i], dom, ydev))
        for dx in (1, 2, 3):
            go(remote(stage.at[i, 1, (x + dx) % NX], pool.at[dev_of(x, yh, zsrc)],
                      xs.at[i, 0, dx], xr.at[i, 0, dx], dom, xdev(dx)))
        go(pltpu.make_async_copy(stage.at[i, 1, x], pool.at[dev_of(x, yh, zsrc)], ls.at[i, 0]))

    def pass_on(rel):
        i = SLOT[rel]
        zsrc = (z + rel + NZ) % NZ
        remote(stage.at[i, 0], relay.at[i], ys.at[i], yr.at[i], dom, ydev).wait_recv()
        for dx in (1, 2, 3):
            go(remote(relay.at[i, (x + dx) % NX], pool.at[dev_of(x, yo, zsrc)],
                      xs.at[i, 1, dx], xr.at[i, 1, dx], dom, xdev(dx)))
        go(pltpu.make_async_copy(relay.at[i, x], pool.at[dev_of(x, yo, zsrc)], ls.at[i, 1]))

    serve(0)
    for rel in RELS[1:]:
        i = SLOT[rel]
        remote(slots_vm, tab_vm.at[i], meta_s.at[i], meta_r.at[i], dom, zdev(rel)).wait_recv()
    tab_vm[0] = slots_vm[...]
    to_sm = pltpu.make_async_copy(tab_vm, tab_sm, ts.at[0])
    to_sm.start()
    to_out = pltpu.make_async_copy(tab_vm, tab, ts.at[1])
    to_out.start()
    to_sm.wait()

    for j in (1, 2, 3):
        for n in (0, 1):
            zcopy(0, -j, n, 1).wait_recv()
            if j < 3:
                go(zcopy(-j, -j - 1, n, 1))
            elif n == 0:
                go(zcopy(-3, 4, 0, 1))
            zcopy(0, j, 1 - n, -1).wait_recv()
            if j < 3:
                go(zcopy(j, j + 1, 1 - n, -1))
            elif n == 0:
                go(zcopy(3, 4, 1, -1))
        serve(-j)
        serve(j)
        if j == 1:
            pass_on(0)
            remote(feat, rem.at[1], ds.at[1], dr.at[1], far, dev).wait_recv()
            o_far = (sib - far - 1 + 2 * N_DOM) % N_DOM
            go(remote(rem.at[1], rem.at[o_far], ds.at[2], dr.at[2], sib, dev))
        else:
            pass_on(1 - j)
            pass_on(j - 1)
    zcopy(0, 4, 0, 1).wait_recv()
    zcopy(0, 4, 1, -1).wait_recv()
    serve(4)
    pass_on(-3)
    pass_on(3)
    pass_on(4)

    remote(feat, rem.at[o_sib], ds.at[0], dr.at[0], sib, dev).wait_recv()
    remote(feat, rem.at[o_sib], ds.at[2], dr.at[2], sib, dev).wait_recv()
    for rel in RELS:
        i = SLOT[rel]
        for g in (0, 1):
            for dx in (1, 2, 3):
                remote(relay.at[0, 0], pool.at[0], xs.at[i, g, dx], xr.at[i, g, dx], dom, xdev(dx)).wait_recv()
    for copy in live:
        if hasattr(copy, "wait_send") and copy.is_remote:
            copy.wait_send()
        else:
            copy.wait()
    to_out.wait()


def gather(features, send_row):
    vm = pl.BlockSpec(memory_space=pltpu.VMEM)
    sm = pl.BlockSpec(memory_space=pltpu.SMEM)
    hbm = pl.BlockSpec(memory_space=pl.ANY)
    dma = pltpu.SemaphoreType.DMA
    padded = jnp.zeros((8, 128), jnp.int32).at[0, : send_row.shape[0]].set(send_row)
    return pl.pallas_call(
        gather_kernel,
        out_shape=(
            jax.ShapeDtypeStruct((NX * NY * NZ, BLK, F), BF),
            jax.ShapeDtypeStruct((N_DOM - 1, RB, BLK, F), BF),
            jax.ShapeDtypeStruct((NZ, 8, 128), jnp.int32),
        ),
        in_specs=[vm, sm, vm],
        out_specs=(hbm, hbm, hbm),
        scratch_shapes=[pltpu.VMEM((RB, BLK, F), BF)] * 7 + [
            pltpu.VMEM((NZ, 2, NX, BLK, F), BF),
            pltpu.VMEM((NZ, NX, BLK, F), BF),
            pltpu.VMEM((NZ, 8, 128), jnp.int32),
            pltpu.SMEM((NZ, 8, 128), jnp.int32),
            dma((NZ,)), dma((NZ,)),
            dma((2 * NZ,)), dma((2 * NZ,)),
            dma((NZ, 2, 4)), dma((NZ, 2, 4)),
            dma((NZ,)), dma((NZ,)),
            dma((NZ, 2)),
            dma((3,)), dma((3,)),
            dma((2,)),
        ],
        compiler_params=pltpu.CompilerParams(
            collective_id=0, has_side_effects=True, vmem_limit_bytes=40 << 20),
        name="gather_blocks",
    )(features, send_row, padded)


def layer_kernel(rows_sm, src_sm, count_sm, crow_sm, ccol_sm, pool, rem, ivals, cvals, w, cot,
                 act, sums, csums, wpart, acc, back, slots, cacc):
    count = count_sm[0, 0]
    acc[...] = jnp.zeros_like(acc)

    for o in range(N_DOM - 1):
        def cross(k4, carry, o=o):
            for u in range(4):
                k = k4 * 4 + u
                acc[crow_sm[0, 0, o, k]] += jnp.dot(
                    cvals[o, k], rem[o, ccol_sm[0, 0, o, k]], preferred_element_type=F32)
            return carry
        lax.fori_loop(0, KX // 4, cross, 0)

    def intra(k4, carry):
        for u in range(4):
            k = k4 * 4 + u
            part = jnp.dot(ivals[k], pool[src_sm[0, 0, k]], preferred_element_type=F32)
            acc[rows_sm[0, 0, k]] += jnp.where(k < count, part, 0.0)
        return carry
    lax.fori_loop(0, (count + 3) // 4, intra, 0)

    wpart[...] = jnp.zeros_like(wpart)

    def dense(r, carry):
        agg = acc[r].astype(BF)
        pre = jnp.dot(agg, w[...], preferred_element_type=F32)
        sig = jax.nn.sigmoid(pre)
        act[r] = (pre * sig).astype(BF)
        grad = (cot[r].astype(F32) * sig * (1.0 + pre * (1.0 - sig))).astype(BF)
        wpart[...] += lax.dot_general(agg, grad, (((0,), (0,)), ((), ())), preferred_element_type=F32)
        back[r] = lax.dot_general(
            grad, w[...], (((1,), (1,)), ((), ())), preferred_element_type=F32).astype(BF)
        return carry
    lax.fori_loop(0, RB, dense, 0)

    slots[...] = jnp.zeros_like(slots)
    cacc[...] = jnp.zeros_like(cacc)
    turned = (((0,), (0,)), ((), ()))

    def intra_back(k4, carry):
        for u in range(4):
            k = k4 * 4 + u
            part = lax.dot_general(ivals[k], back[rows_sm[0, 0, k]], turned, preferred_element_type=F32)
            slots[src_sm[0, 0, k]] += jnp.where(k < count, part, 0.0)
        return carry
    lax.fori_loop(0, (count + 3) // 4, intra_back, 0)

    for o in range(N_DOM - 1):
        def cross_back(k4, carry, o=o):
            for u in range(4):
                k = k4 * 4 + u
                cacc[o, ccol_sm[0, 0, o, k]] += lax.dot_general(
                    cvals[o, k], back[crow_sm[0, 0, o, k]], turned, preferred_element_type=F32)
            return carry
        lax.fori_loop(0, KX // 4, cross_back, 0)

    def narrow(i, carry):
        sums[i] = slots[i].astype(BF)
        return carry
    lax.fori_loop(0, NX * NY * NZ, narrow, 0)
    for o in range(N_DOM - 1):
        for b in range(RB):
            csums[o, b] = cacc[o, b].astype(BF)


def layer(rows, src, count, crow, ccol, pool, rem, ivals, cvals, w, cot):
    vm = pl.BlockSpec(memory_space=pltpu.VMEM)
    sm = pl.BlockSpec(memory_space=pltpu.SMEM)
    n = NX * NY * NZ
    return pl.pallas_call(
        layer_kernel,
        out_shape=(
            jax.ShapeDtypeStruct((RB, BLK, F), BF),
            jax.ShapeDtypeStruct((n, BLK, F), BF),
            jax.ShapeDtypeStruct((N_DOM - 1, RB, BLK, F), BF),
            jax.ShapeDtypeStruct((F, F), F32),
        ),
        in_specs=[sm] * 5 + [vm] * 6,
        out_specs=(vm, vm, vm, vm),
        scratch_shapes=[
            pltpu.VMEM((RB, BLK, F), F32),
            pltpu.VMEM((RB, BLK, F), BF),
            pltpu.VMEM((n, BLK, F), F32),
            pltpu.VMEM((N_DOM - 1, RB, BLK, F), F32),
        ],
        compiler_params=pltpu.CompilerParams(vmem_limit_bytes=56 << 20),
        name="layer_tiles",
    )(rows, src, count, crow, ccol, pool, rem, ivals, cvals, w, cot)


BACK_RELS = (4, 3, -3, 2, -2, 1, -1, 0)
STRIP = 16
W_SCALE = 1.0 / math.sqrt(RB * BLK * NX * NY * NZ * N_DOM)


def scatter_kernel(sums, csums, tab, wpart, out, wg,
                   xbuf, ybuf, part, rin, lin, near, far_in, pair, far_got, wquarter, wplane, wline,
                   xs, xr, ls, ys, yr, rs, rr, lts, ltr, ds, dr, ws, wr):
    dom, dev, x, yh, z = position()
    yo = 1 - yh
    place = x * NY + yh

    def zdev(rel):
        return dev_of(x, yh, (z + rel + NZ) % NZ)

    def xdev(dx):
        return dev_of((x + dx) % NX, yh, z)

    ydev = dev_of(x, yo, z)
    sib = dom + 1 - 2 * (dom % 2)
    far = (dom + 2) % N_DOM
    sib_far = (sib + 2) % N_DOM

    def o_of(target):
        return (dom - target - 1 + 2 * N_DOM) % N_DOM

    plane = [(dx, dy) for dy in (0, 1) for dx in range(NX) if dx or dy]

    def pdev(dx, dy):
        return dev_of((x + dx) % NX, (yh + dy) % NY, z)

    greet([(dom, zdev(rel)) for rel in RELS[1:]] + [(dom, pdev(dx, dy)) for dx, dy in plane]
          + [(sib, dev), (far, dev), (sib_far, dev)])

    live = []

    def go(copy):
        copy.start()
        live.append(copy)
        return copy

    doms = (sib, far, sib_far)
    wrows = F // N_DOM
    first = dom * wrows + place * 8

    def w_dom(n):
        return remote(wpart.at[pl.ds(doms[n] * wrows, wrows)], wquarter.at[n], ws.at[n], wr.at[n], doms[n], dev)

    def w_plane(n):
        dx, dy = plane[n]
        there = ((x + dx) % NX) * NY + (yh + dy) % NY
        return remote(wquarter.at[3, pl.ds(there * 8, 8)], wplane.at[n], ws.at[3 + n], wr.at[3 + n],
                      dom, pdev(dx, dy))

    def w_line(n):
        return remote(wplane.at[7], wline.at[z], ws.at[10 + n], wr.at[10 + n], dom, zdev(RELS[1 + n]))

    def w_plane_back(n):
        dx, dy = plane[n]
        rows = pl.ds(first, 8)
        return remote(wg.at[rows], wg.at[rows], ws.at[17 + n], wr.at[17 + n], dom, pdev(dx, dy))

    def w_dom_back(n):
        rows = pl.ds(dom * wrows, wrows)
        return remote(wg.at[rows], wg.at[rows], ws.at[24 + n], wr.at[24 + n], doms[n], dev)

    def w_step(step):
        if step == 0:
            for n in range(3):
                go(w_dom(n))
        if step == 1:
            for n in range(3):
                w_dom(n).wait_recv()
            wquarter[3] = (wpart[pl.ds(dom * wrows, wrows)] + wquarter[0]) + (wquarter[1] + wquarter[2])
            for n in range(7):
                go(w_plane(n))
        if step == 2:
            for n in range(7):
                w_plane(n).wait_recv()
            total = wquarter[3, pl.ds(place * 8, 8)]
            for n in range(7):
                total = total + wplane[n]
            wplane[7] = total
            wline[z] = total
            for n in range(7):
                go(w_line(n))
        if step == 3:
            for n in range(7):
                w_line(n).wait_recv()
            total = wline[0]
            for n in range(1, NZ):
                total = total + wline[n]
            wg[pl.ds(first, 8)] = total * W_SCALE
            for n in range(7):
                go(w_plane_back(n))
        if step == 4:
            for n in range(7):
                w_plane_back(n).wait_recv()
            for n in range(3):
                go(w_dom_back(n))
        if step == 5:
            for n in range(3):
                w_dom_back(n).wait_recv()

    go(remote(csums.at[o_of(sib_far)], pair, ds.at[0], dr.at[0], sib, dev))
    go(remote(csums.at[o_of(sib)], near, ds.at[1], dr.at[1], sib, dev))

    def xsend(rel):
        i = SLOT[rel]
        zdst = (z + rel + NZ) % NZ
        for dx in (1, 2, 3):
            go(remote(sums.at[(x + dx) % NX, :, zdst], xbuf.at[i, dx], xs.at[i, dx], xr.at[i, dx],
                      dom, xdev(dx)))
        own = pltpu.make_async_copy(sums.at[x, :, zdst], xbuf.at[i, 0], ls.at[i])
        own.start()

    def ysend(rel):
        i = SLOT[rel]
        zdst = (z + rel + NZ) % NZ
        for dx in (1, 2, 3):
            remote(sums.at[0, :, 0], xbuf.at[i, dx], xs.at[i, dx], xr.at[i, dx], dom, xdev(dx)).wait_recv()
        pltpu.make_async_copy(sums.at[x, :, zdst], xbuf.at[i, 0], ls.at[i]).wait()
        go(remote(xbuf.at[i, :, yo], ybuf.at[i], ys.at[i], yr.at[i], dom, ydev))

    def ywait(rel):
        i = SLOT[rel]
        remote(xbuf.at[i, :, yo], ybuf.at[i], ys.at[i], yr.at[i], dom, ydev).wait_recv()

    def combine(rel, extra, store):
        i = SLOT[rel]
        picks = []
        for g, y in ((0, yh), (1, yo)):
            for dx in range(NX):
                d = dev_of((x - dx + NX) % NX, y, z)
                pick = tab[i, 0, d]
                picks.append((g, dx, [jnp.where(pick == b, 1.0, 0.0).astype(F32) for b in range(RB)]))

        def strip(s, carry):
            rows = pl.ds(pl.multiple_of(s * STRIP, STRIP), STRIP)
            totals = [None] * RB
            for g, dx, on in picks:
                got = (xbuf[i, dx, yh, rows] if g == 0 else ybuf[i, dx, rows]).astype(F32)
                for b in range(RB):
                    term = got * on[b]
                    totals[b] = term if totals[b] is None else totals[b] + term
            for b in range(RB):
                total = totals[b]
                for ref, blocks in extra:
                    if b in blocks:
                        total = total + ref[b, rows].astype(F32)
                store[b, rows] = total.astype(BF)
            return carry
        lax.fori_loop(0, BLK // STRIP, strip, 0)

    every = tuple(range(RB))
    low, high = every[:HALF], every[HALF:]

    def rcopy(src_rel, j):
        i = SLOT[src_rel]
        if j == 3:
            a = pl.ds(0, HALF)
            return remote(part.at[i, a], rin.at[j, a], rs.at[j], rr.at[j], dom, zdev(1))
        return remote(part.at[i], rin.at[j], rs.at[j], rr.at[j], dom, zdev(1))

    def lcopy(src_rel, j):
        i = SLOT[src_rel]
        if j == 3:
            a = pl.ds(HALF, HALF)
            return remote(part.at[i, a], lin.at[j, a], lts.at[j], ltr.at[j], dom, zdev(-1))
        return remote(part.at[i], lin.at[j], lts.at[j], ltr.at[j], dom, zdev(-1))

    w_step(0)
    xsend(4)
    xsend(3)
    xsend(-3)
    remote(csums.at[0], pair, ds.at[0], dr.at[0], sib, dev).wait_recv()

    def add_pair(b, carry):
        far_in[b] = (pair[b].astype(F32) + csums[o_of(far), b].astype(F32)).astype(BF)
        return carry
    lax.fori_loop(0, RB, add_pair, 0)
    w_step(1)
    ysend(4)
    xsend(2)
    xsend(-2)
    ysend(3)
    ysend(-3)
    go(remote(far_in, far_got, ds.at[2], dr.at[2], far, dev))
    ywait(4)
    combine(4, [], part.at[SLOT[4]])
    go(rcopy(4, 3))
    go(lcopy(4, 3))
    w_step(2)
    for j in (3, 2, 1):
        if j == 3:
            xsend(1)
            xsend(-1)
        if j == 2:
            xsend(0)
        if j > 1:
            ysend(j - 1)
            ysend(1 - j)
        else:
            ysend(0)
        ywait(j)
        rcopy(4, j).wait_recv()
        combine(j, [(rin.at[j], low if j == 3 else every)], part.at[SLOT[j]])
        go(rcopy(j, j - 1))
        ywait(-j)
        lcopy(4, j).wait_recv()
        combine(-j, [(lin.at[j], high if j == 3 else every)], part.at[SLOT[-j]])
        go(lcopy(-j, j - 1))
        w_step(6 - j)
    ywait(0)
    remote(csums.at[0], near, ds.at[1], dr.at[1], sib, dev).wait_recv()
    remote(far_in, far_got, ds.at[2], dr.at[2], far, dev).wait_recv()
    rcopy(4, 0).wait_recv()
    lcopy(4, 0).wait_recv()
    combine(0, [(rin.at[0], every), (lin.at[0], every), (near, every), (far_got, every)], out)
    for copy in live:
        copy.wait_send()


def scatter(sums, csums, tab, wpart):
    vm = pl.BlockSpec(memory_space=pltpu.VMEM)
    sm = pl.BlockSpec(memory_space=pltpu.SMEM)
    dma = pltpu.SemaphoreType.DMA
    block = (RB, BLK, F)
    return pl.pallas_call(
        scatter_kernel,
        out_shape=(jax.ShapeDtypeStruct(block, BF), jax.ShapeDtypeStruct((F, F), F32)),
        in_specs=[vm, vm, sm, vm],
        out_specs=(vm, vm),
        scratch_shapes=[
            pltpu.VMEM((NZ, NX, NY, BLK, F), BF),
            pltpu.VMEM((NZ, NX, BLK, F), BF),
            pltpu.VMEM((NZ,) + block, BF),
            pltpu.VMEM((4,) + block, BF),
            pltpu.VMEM((4,) + block, BF),
            pltpu.VMEM(block, BF), pltpu.VMEM(block, BF), pltpu.VMEM(block, BF), pltpu.VMEM(block, BF),
            pltpu.VMEM((4, F // N_DOM, F), F32), pltpu.VMEM((8, 8, F), F32), pltpu.VMEM((NZ, 8, F), F32),
            dma((NZ, 4)), dma((NZ, 4)), dma((NZ,)),
            dma((NZ,)), dma((NZ,)),
            dma((4,)), dma((4,)), dma((4,)), dma((4,)),
            dma((3,)), dma((3,)),
            dma((27,)), dma((27,)),
        ],
        compiler_params=pltpu.CompilerParams(
            collective_id=1, has_side_effects=True, vmem_limit_bytes=48 << 20),
        name="scatter_sums",
    )(sums.reshape(NX, NY, NZ, BLK, F), csums, tab, wpart)


def body(features, weight, cotangent, send_list, intra_rows, intra_src, intra_count, intra_vals,
         cross_rows, cross_cols, cross_vals):
    own = features.reshape(RB, BLK, F)
    pool, rem, tab = gather(own, send_list.reshape(-1))
    act, sums, csums, wpart = layer(
        intra_rows, intra_src, intra_count, cross_rows, cross_cols, pool, rem,
        intra_vals[0, 0], cross_vals[0, 0], weight, cotangent.reshape(RB, BLK, F))
    input_grad, weight_grad = scatter(sums, csums, tab, wpart)
    return act.reshape(RB * BLK, F), input_grad.reshape(RB * BLK, F), weight_grad


def solution(mesh):
    placed = (
        P(("dom", "dev"), None),
        P(),
        P(("dom", "dev"), None),
        P("dom", "dev", None, None),
        P("dom", "dev", None),
        P("dom", "dev", None),
        P("dom", "dev"),
        P("dom", "dev", None, None, None),
        P("dom", "dev", None, None),
        P("dom", "dev", None, None),
        P("dom", "dev", None, None, None, None),
    )
    return jax.shard_map(
        body,
        mesh=mesh,
        in_specs=placed,
        out_specs=(P(("dom", "dev"), None), P(("dom", "dev"), None), P()),
        check_vma=False,
    )
```

```python
import math

import jax
import jax.numpy as jnp
from jax import lax
from jax.experimental import pallas as pl
from jax.experimental.pallas import tpu as pltpu
from jax.sharding import PartitionSpec as P

MESH = pl.DeviceIdType.MESH
BF = jnp.bfloat16
F32 = jnp.float32
I32 = jnp.int32
NX, NY, NZ = 4, 2, 8
RB, BLK, F = 8, 128, 256
HW = F // 2
N_DOM = 4
KIN, KX = 32, 16
NCROSS = (N_DOM - 1) * KX
W_SCALE = 1.0 / math.sqrt(RB * BLK * NX * NY * NZ * N_DOM)
STRIP = 32
RELS = (0, -1, 1, -2, 2, -3, 3, 4)
SLOT = {rel: i for i, rel in enumerate(RELS)}
SEND, IROW, ISRC, ICOUNT, CROW, CCOL = 0, 1, 2, 3, 8, 11
POS_A, POS_B, POS_C, POS_D, N_POS = 0, 48, 80, 112, 160
KEY_A, KEY_B, KEY_C, KEY_D = 0, 32, 64, 160


def dev_of(x, yh, z):
    return x * 16 + yh * 8 + z


def remote(src, dst, send_sem, recv_sem, dom, dev):
    return pltpu.make_async_remote_copy(
        src_ref=src, dst_ref=dst, send_sem=send_sem, recv_sem=recv_sem,
        device_id=(dom, dev), device_id_type=MESH)


def order_tiles(ints, key_rows, found):
    count = ints[ICOUNT, 0]
    lane = lax.broadcasted_iota(I32, (8, 256), 1)
    keys_lane = jnp.full((8, 256), 9999, I32)

    def put(e, key, keys_lane):
        key_rows[pl.ds(e, 1), :] = jnp.full((1, 256), key, I32)
        return jnp.where(lane == e, key, keys_lane)

    def cross(e, keys_lane):
        o = e // KX
        keys_lane = put(POS_A + e, KEY_A + o * RB + ints[CROW + e // KX, e % KX], keys_lane)
        return put(POS_D + e, KEY_D + o * RB + ints[CCOL + e // KX, e % KX], keys_lane)

    def intra(k, keys_lane):
        keys_lane = put(POS_B + k, KEY_B + jnp.where(k < count, ints[IROW, k], RB), keys_lane)
        return put(POS_C + k, KEY_C + jnp.where(k < count, ints[ISRC, k], NX * NY * NZ), keys_lane)

    keys_lane = lax.fori_loop(0, NCROSS, cross, keys_lane)
    keys_lane = lax.fori_loop(0, KIN, intra, keys_lane)

    def step(t, sums):
        tile, le, eq, skey = sums
        base = pl.multiple_of(t * 8, 8)
        rows = key_rows[pl.ds(base, 8), :]
        sub = base + lax.broadcasted_iota(I32, (8, 256), 0)
        ahead = (keys_lane < rows) | ((keys_lane == rows) & (lane < sub))
        place = jnp.sum(jnp.where(ahead, 1, 0), axis=1, keepdims=True)
        here = place == lane
        tile = tile + jnp.where(here, sub, 0)
        skey = skey + jnp.where(here, rows, 0)
        le = le + jnp.where(rows <= lane, 1, 0)
        eq = eq + jnp.where(rows == lane, 1, 0)
        return tile, le, eq, skey

    zero = jnp.zeros((8, 256), I32)
    tile, le, eq, skey = lax.fori_loop(0, N_POS // 8, step, (zero, zero, zero, zero))
    for r, value in enumerate((tile, le, eq, skey)):
        found[r] = jnp.broadcast_to(jnp.sum(value, axis=0, keepdims=True), (8, 256))


def kernel(ints, ints_vm, feat_hbm, ivals_hbm, cvals_hbm, w, cot_hbm,
           act_hbm, out, wg,
           *scr):
    it = iter(scr)
    feat = next(it)
    own = (next(it), next(it))
    bufs = {0: own}
    for rel in RELS[1:]:
        bufs[rel] = (next(it), next(it))
    (stage, relay, pool, rem_sib, rem_far, rem_sf, ivals, cvals, cot, act, agg, grad, back,
     runs_a, runs_b, key_rows, found, found_sm, tab_vm, tab_sm,
     xbuf, ybuf, part, rin, lin, csums, near, pair, far_in, far_got, wpart, wquarter, wplane, wline,
     loc, meta_s, meta_r, zs, zr, xs, xr, ys, yr, ls, ds, dr,
     bxs, bxr, bls, bys, byr, rs, rr, lts, ltr, bds, bdr, ws, wr) = it
    dom = lax.axis_index("dom")
    dev = lax.axis_index("dev")
    x, yh, z = dev // 16, (dev // 8) % 2, dev % 8
    yo = 1 - yh
    here = x * NY + yh

    def zdev(rel):
        return dev_of(x, yh, (z + rel + NZ) % NZ)

    def xdev(dx):
        return dev_of((x + dx) % NX, yh, z)

    plane = [(dx, dy) for dy in (0, 1) for dx in range(NX) if dx or dy]

    def pdev(dx, dy):
        return dev_of((x + dx) % NX, (yh + dy) % NY, z)

    ydev = dev_of(x, yo, z)
    sib = dom + 1 - 2 * (dom % 2)
    far = (dom + 2) % N_DOM
    sf = (sib + 2) % N_DOM
    doms = (sib, far, sf)

    def o_of(other):
        return (dom - other - 1 + 2 * N_DOM) % N_DOM

    loads = []

    def load(src, dst):
        copy = pltpu.make_async_copy(src, dst, loc.at[len(loads)])
        copy.start()
        loads.append(copy)
        return copy

    to_half = [load(feat_hbm.at[:, :, pl.ds(h * HW, HW)], own[h]) for h in (0, 1)]
    to_feat = load(feat_hbm, feat)
    to_cvals = load(cvals_hbm, cvals)
    to_ivals = load(ivals_hbm, ivals)
    to_cot = load(cot_hbm, cot)

    peers = ([(dom, zdev(rel)) for rel in RELS[1:]] + [(dom, pdev(dx, dy)) for dx, dy in plane]
             + [(d, dev) for d in doms])
    barrier = pltpu.get_barrier_semaphore()
    for d, e in peers:
        pl.semaphore_signal(barrier, inc=1, device_id=(d, e), device_id_type=MESH)
    to_half[0].wait()
    to_half[1].wait()
    pl.semaphore_wait(barrier, len(peers))

    live = []

    def go(copy):
        copy.start()
        live.append(copy)

    def zcopy(src_rel, dst_rel, h):
        s = SLOT[dst_rel] * 2 + h
        to = 1 if dst_rel < 0 or (dst_rel == 4 and h == 0) else -1
        return remote(bufs[src_rel][h], bufs[dst_rel][h], zs.at[s], zr.at[s], dom, zdev(to))

    def zarrived(rel, h):
        zcopy(0, rel, h).wait_recv()

    def meta(rel):
        i = SLOT[-rel] if rel != 4 else SLOT[4]
        return remote(ints_vm.at[pl.ds(0, 8)], tab_vm.at[i], meta_s.at[i], meta_r.at[i], dom, zdev(rel))

    def dcopy(n):
        if n == 0:
            return remote(feat, rem_sib, ds.at[0], dr.at[0], sib, dev)
        if n == 1:
            return remote(feat, rem_far, ds.at[1], dr.at[1], far, dev)
        return remote(rem_far, rem_sf, ds.at[2], dr.at[2], sib, dev)

    def ycopy(rel, h):
        i = SLOT[rel]
        return remote(stage.at[i, h, 0], relay.at[i, h], ys.at[i, h], yr.at[i, h], dom, ydev)

    def serve(rel, h):
        i = SLOT[rel]
        buf = bufs[rel][h]
        zsrc = (z + rel + NZ) % NZ
        for g, y in ((0, yo), (1, yh)):
            for xx in range(NX):
                where = dev_of(xx, y, z)
                pick = ints[SEND, where] if rel == 0 else tab_sm[i, SEND, where]
                stage[i, h, g, xx] = buf[pick]
            if g == 0:
                go(ycopy(rel, h))
        for dx in (1, 2, 3):
            go(remote(stage.at[i, h, 1, (x + dx) % NX], pool.at[h, x, yh, zsrc],
                      xs.at[i, h, 0, dx], xr.at[i, h, 0, dx], dom, xdev(dx)))
        go(pltpu.make_async_copy(stage.at[i, h, 1, x], pool.at[h, x, yh, zsrc], ls.at[i, h, 0]))

    def pass_on(rel, h):
        i = SLOT[rel]
        zsrc = (z + rel + NZ) % NZ
        ycopy(rel, h).wait_recv()
        for dx in (1, 2, 3):
            go(remote(relay.at[i, h, (x + dx) % NX], pool.at[h, x, yo, zsrc],
                      xs.at[i, h, 1, dx], xr.at[i, h, 1, dx], dom, xdev(dx)))
        go(pltpu.make_async_copy(relay.at[i, h, x], pool.at[h, x, yo, zsrc], ls.at[i, h, 1]))

    for h in (0, 1):
        go(zcopy(0, -1, h))
        go(zcopy(0, 1, 1 - h))
    serve(0, 0)
    serve(0, 1)
    for rel in RELS[1:]:
        go(meta(rel))
    to_feat.wait()
    go(dcopy(0))
    go(dcopy(1))

    order_tiles(ints, key_rows, found)
    to_found = load(found, found_sm)
    runs_a[0] = jnp.zeros((BLK, F), F32)
    runs_b[0] = jnp.zeros((BLK, F), F32)

    for rel in RELS[1:]:
        meta(rel).wait_recv()
    tab_vm[0] = ints_vm[:8]
    to_tab = load(tab_vm, tab_sm)
    to_found.wait()
    to_tab.wait()

    def tile_at(i):
        return found_sm[0, 0, i]

    def joined(i, before, product):
        same = (i > 0) & (found_sm[3, 0, i] == found_sm[3, 0, jnp.maximum(i - 1, 0)])
        return product + jnp.where(same, before, 0.0)

    def cross_forward(rem, o, half):
        def step(u4, carry):
            for u in range(4):
                i = o * KX + half * (KX // 2) + u4 * 4 + u
                e = tile_at(POS_A + i)
                product = jnp.dot(cvals[e], rem[ints[CCOL + e // KX, e % KX]], preferred_element_type=F32)
                runs_a[i + 1] = joined(POS_A + i, runs_a[i], product)
            return carry
        lax.fori_loop(0, KX // 8, step, 0)

    to_cvals.wait()
    items = [(s * j, h if s < 0 else 1 - h) for j in (1, 2, 3) for h in (0, 1) for s in (-1, 1)]
    items = [(0, 0), (0, 1)] + items + [(4, 0), (4, 1)]
    LAG = 3
    for n in range(2, len(items) + LAG):
        if n < len(items):
            rel, h = items[n]
            zarrived(rel, h)
            if rel != 4:
                nxt = rel - 1 if rel < 0 else rel + 1
                if nxt == -4 and h == 0:
                    go(zcopy(rel, 4, 0))
                elif nxt == 4 and h == 1:
                    go(zcopy(rel, 4, 1))
                elif abs(nxt) < 4:
                    go(zcopy(rel, nxt, h))
            serve(rel, h)
        if n - LAG >= 0:
            pass_on(*items[n - LAG])
        if n == 4:
            dcopy(0).wait_recv()
        if n == 6:
            dcopy(1).wait_recv()
            go(dcopy(2))
        if n == 9:
            dcopy(2).wait_recv()
        if n in (4, 5):
            cross_forward(rem_sib, o_of(sib), n - 4)
        if n in (7, 8):
            cross_forward(rem_far, o_of(far), n - 7)
        if n in (10, 11):
            cross_forward(rem_sf, o_of(sf), n - 10)

    for rel, h in items:
        i = SLOT[rel]
        for g in (0, 1):
            for dx in (1, 2, 3):
                remote(relay.at[0, 0, 0], pool.at[0, 0, 0, 0], xs.at[i, h, g, dx], xr.at[i, h, g, dx],
                       dom, xdev(dx)).wait_recv()
    for copy in live:
        if copy.is_remote:
            copy.wait_send()
        else:
            copy.wait()
    live.clear()
    to_ivals.wait()
    to_cot.wait()

    def intra_forward(u4, carry):
        for u in range(4):
            i = u4 * 4 + u
            k = tile_at(POS_B + i) - POS_B
            src = ints[ISRC, k]
            sx, sy, sz = src // 16, (src // 8) % 2, src % 8
            picked = jnp.concatenate([pool[0, sx, sy, sz], pool[1, sx, sy, sz]], axis=1)
            product = jnp.dot(ivals[k], picked, preferred_element_type=F32)
            runs_b[i + 1] = joined(POS_B + i, runs_b[i], product)
        return carry
    lax.fori_loop(0, KIN // 4, intra_forward, 0)

    def run_of(runs, key, first):
        last = jnp.maximum(found_sm[1, 0, key] - first, 0)
        return jnp.where(found_sm[2, 0, key] > 0, runs[last], 0.0)

    def dense(r, carry):
        total = run_of(runs_b, KEY_B + r, POS_B)
        for o in range(N_DOM - 1):
            total = total + run_of(runs_a, KEY_A + o * RB + r, POS_A)
        agg_r = total.astype(BF)
        agg[r] = agg_r
        pre = jnp.dot(agg_r, w[...], preferred_element_type=F32)
        sig = jax.nn.sigmoid(pre)
        act[r] = (pre * sig).astype(BF)
        grad_r = (cot[r].astype(F32) * sig * (1.0 + pre * (1.0 - sig))).astype(BF)
        grad[r] = grad_r
        back[r] = lax.dot_general(
            grad_r, w[...], (((1,), (1,)), ((), ())), preferred_element_type=F32).astype(BF)
        return carry
    lax.fori_loop(0, RB, dense, 0)

    turned = (((0,), (0,)), ((), ()))

    def intra_back(u4, carry):
        for u in range(4):
            i = u4 * 4 + u
            k = tile_at(POS_C + i) - POS_C
            product = lax.dot_general(ivals[k], back[ints[IROW, k]], turned, preferred_element_type=F32)
            runs_b[i + 1] = joined(POS_C + i, runs_b[i], product)
        return carry
    lax.fori_loop(0, KIN // 4, intra_back, 0)

    def fill(rel):
        zdst = (z + rel + NZ) % NZ

        def one(c, carry):
            total = run_of(runs_b, KEY_C + (c // NY) * 16 + (c % NY) * 8 + zdst, POS_C).astype(BF)
            pool[0, c // NY, c % NY, zdst] = total[:, :HW]
            pool[1, c // NY, c % NY, zdst] = total[:, HW:]
            return carry
        lax.fori_loop(0, NX * NY, one, 0)

    def bxcopy(rel, h, dx):
        i = SLOT[rel]
        zdst = (z + rel + NZ) % NZ
        return remote(pool.at[h, (x + dx) % NX, :, zdst], xbuf.at[i, h, dx], bxs.at[i, h, dx],
                      bxr.at[i, h, dx], dom, xdev(dx))

    def bown(rel, h):
        i = SLOT[rel]
        zdst = (z + rel + NZ) % NZ
        return pltpu.make_async_copy(pool.at[h, x, :, zdst], xbuf.at[i, h, 0], bls.at[i, h])

    def xsend(rel, h):
        for dx in (1, 2, 3):
            go(bxcopy(rel, h, dx))
        bown(rel, h).start()

    def bycopy(rel, h):
        i = SLOT[rel]
        return remote(xbuf.at[i, h, :, yo], ybuf.at[i, h], bys.at[i, h], byr.at[i, h], dom, ydev)

    def ysend(rel, h):
        for dx in (1, 2, 3):
            bxcopy(rel, h, dx).wait_recv()
        bown(rel, h).wait()
        go(bycopy(rel, h))

    def rcopy(src_rel, j, h):
        return remote(part.at[SLOT[src_rel], h], rin.at[j, h], rs.at[j, h], rr.at[j, h], dom, zdev(1))

    def lcopy(src_rel, j, h):
        return remote(part.at[SLOT[src_rel], h], lin.at[j, h], lts.at[j, h], ltr.at[j, h], dom, zdev(-1))

    def combine(rel, h, extra, store):
        i = SLOT[rel]
        bycopy(rel, h).wait_recv()
        picks = []
        for g, y in ((0, yh), (1, yo)):
            for dx in range(NX):
                d = dev_of((x - dx + NX) % NX, y, z)
                pick = tab_sm[i, SEND, d]
                picks.append((g, dx, [jnp.where(pick == b, 1.0, 0.0).astype(F32) for b in range(RB)]))

        def strip(s, carry):
            rows = pl.ds(pl.multiple_of(s * STRIP, STRIP), STRIP)
            totals = [None] * RB
            for g, dx, on in picks:
                got = (xbuf[i, h, dx, yh, rows] if g == 0 else ybuf[i, h, dx, rows]).astype(F32)
                for b in range(RB):
                    term = got * on[b]
                    totals[b] = term if totals[b] is None else totals[b] + term
            for b in range(RB):
                total = totals[b]
                for ref in extra:
                    total = total + ref[b, rows].astype(F32)
                store(b, rows, total.astype(BF))
            return carry
        lax.fori_loop(0, BLK // STRIP, strip, 0)

    def into_part(rel, h):
        def store(b, rows, value):
            part[SLOT[rel], h, b, rows] = value
        return store

    def cross_back(other):
        o = o_of(other)

        def step(u4, carry):
            for u in range(4):
                i = o * KX + u4 * 4 + u
                e = tile_at(POS_D + i) - POS_D
                product = lax.dot_general(cvals[e], back[ints[CROW + e // KX, e % KX]], turned, preferred_element_type=F32)
                runs_a[i + 1] = joined(POS_D + i, runs_a[i], product)
            return carry
        lax.fori_loop(0, KX // 4, step, 0)

        def one(b, carry):
            csums[o, b] = run_of(runs_a, KEY_D + o * RB + b, POS_D).astype(BF)
            return carry
        lax.fori_loop(0, RB, one, 0)

    wrows = F // N_DOM
    first = dom * wrows + here * 8

    def w_dom(n):
        return remote(wpart.at[pl.ds(doms[n] * wrows, wrows)], wquarter.at[n], ws.at[n], wr.at[n], doms[n], dev)

    def w_plane(n):
        dx, dy = plane[n]
        there = ((x + dx) % NX) * NY + (yh + dy) % NY
        return remote(wquarter.at[3, pl.ds(there * 8, 8)], wplane.at[n], ws.at[3 + n], wr.at[3 + n],
                      dom, pdev(dx, dy))

    def w_line(n):
        return remote(wplane.at[7], wline.at[z], ws.at[10 + n], wr.at[10 + n], dom, zdev(RELS[1 + n]))

    def w_plane_back(n):
        dx, dy = plane[n]
        rows = pl.ds(first, 8)
        return remote(wg.at[rows], wg.at[rows], ws.at[17 + n], wr.at[17 + n], dom, pdev(dx, dy))

    def w_dom_back(n):
        rows = pl.ds(dom * wrows, wrows)
        return remote(wg.at[rows], wg.at[rows], ws.at[24 + n], wr.at[24 + n], doms[n], dev)

    def w_step(step):
        if step == 0:
            wpart[...] = jnp.zeros_like(wpart)

            def add(r, carry):
                wpart[...] += lax.dot_general(agg[r], grad[r], turned, preferred_element_type=F32)
                return carry
            lax.fori_loop(0, RB, add, 0)
            for n in range(3):
                go(w_dom(n))
        if step == 1:
            for n in range(3):
                w_dom(n).wait_recv()
            wquarter[3] = (wpart[pl.ds(dom * wrows, wrows)] + wquarter[0]) + (wquarter[1] + wquarter[2])
            for n in range(7):
                go(w_plane(n))
        if step == 2:
            for n in range(7):
                w_plane(n).wait_recv()
            total = wquarter[3, pl.ds(here * 8, 8)]
            for n in range(7):
                total = total + wplane[n]
            wplane[7] = total
            wline[z] = total
            for n in range(7):
                go(w_line(n))
        if step == 3:
            for n in range(7):
                w_line(n).wait_recv()
            total = wline[0]
            for n in range(1, NZ):
                total = total + wline[n]
            wg[pl.ds(first, 8)] = total * W_SCALE
            for n in range(7):
                go(w_plane_back(n))
        if step == 4:
            for n in range(7):
                w_plane_back(n).wait_recv()
            for n in range(3):
                go(w_dom_back(n))
        if step == 5:
            for n in range(3):
                w_dom_back(n).wait_recv()

    def bd(n):
        if n == 0:
            return remote(csums.at[o_of(sf)], pair, bds.at[0], bdr.at[0], sib, dev)
        if n == 1:
            return remote(csums.at[o_of(sib)], near, bds.at[1], bdr.at[1], sib, dev)
        return remote(far_in, far_got, bds.at[2], bdr.at[2], far, dev)

    turns = [(4, 0), (4, 1)] + [(s * j, h if s > 0 else 1 - h)
                                for j in (3, 2, 1) for h in (0, 1) for s in (1, -1)] + [(0, 0), (0, 1)]
    n_turns = len(turns)
    filled = set()

    def xgo(n):
        if n >= n_turns:
            return
        rel, h = turns[n]
        if rel not in filled:
            filled.add(rel)
            fill(rel)
        xsend(rel, h)

    def finish(n):
        rel, h = turns[n]
        if rel == 4:
            combine(4, h, [], into_part(4, h))
            go(rcopy(4, 3, 0) if h == 0 else lcopy(4, 3, 1))
        elif rel > 0:
            extra = []
            if rel < 3 or h == 0:
                rcopy(4, rel, h).wait_recv()
                extra = [rin.at[rel, h]]
            combine(rel, h, extra, into_part(rel, h))
            go(rcopy(rel, rel - 1, h))
        elif rel < 0:
            extra = []
            if rel > -3 or h == 1:
                lcopy(4, -rel, h).wait_recv()
                extra = [lin.at[-rel, h]]
            combine(rel, h, extra, into_part(rel, h))
            go(lcopy(rel, -rel - 1, h))
        else:
            rcopy(4, 0, h).wait_recv()
            lcopy(4, 0, h).wait_recv()
            cols = pl.ds(h * HW, HW)

            def store(b, rows, value):
                out[b, rows, cols] = value
            combine(0, h, [rin.at[0, h], lin.at[0, h], near.at[:, :, cols], far_got.at[:, :, cols]], store)

    XAHEAD, YAHEAD = 6, 3
    for n in range(XAHEAD):
        xgo(n)
    to_act = load(act, act_hbm)
    w_step(0)
    ysend(*turns[0])
    cross_back(sf)
    go(bd(0))
    ysend(*turns[1])
    cross_back(far)
    for n in range(2, YAHEAD):
        ysend(*turns[n])
    bd(0).wait_recv()

    def add_pair(b, carry):
        far_in[b] = (pair[b].astype(F32) + csums[o_of(far), b].astype(F32)).astype(BF)
        return carry
    lax.fori_loop(0, RB, add_pair, 0)
    go(bd(2))
    for n in range(n_turns):
        xgo(n + XAHEAD)
        if n + YAHEAD < n_turns:
            ysend(*turns[n + YAHEAD])
        if n == n_turns - 2:
            bd(1).wait_recv()
            bd(2).wait_recv()
        finish(n)
        if n == 1:
            cross_back(sib)
            go(bd(1))
        if n in (3, 5, 7, 9):
            w_step((n - 1) // 2)
    w_step(5)
    for copy in live:
        copy.wait_send()
    to_act.wait()


def run(ints, features, intra_vals, cross_vals, weight, cotangent):
    vm = pl.BlockSpec(memory_space=pltpu.VMEM)
    sm = pl.BlockSpec(memory_space=pltpu.SMEM)
    hbm = pl.BlockSpec(memory_space=pl.ANY)
    dma = pltpu.SemaphoreType.DMA
    block = (RB, BLK, F)
    half = (RB, BLK, HW)
    V = pltpu.VMEM
    return pl.pallas_call(
        kernel,
        out_shape=(
            jax.ShapeDtypeStruct(block, BF),
            jax.ShapeDtypeStruct(block, BF),
            jax.ShapeDtypeStruct((F, F), F32),
        ),
        in_specs=[sm, vm, hbm, hbm, hbm, vm, hbm],
        out_specs=(hbm, vm, vm),
        scratch_shapes=[V(block, BF)] + [V(half, BF)] * 16 + [
            V((NZ, 2, NY, NX, BLK, HW), BF),
            V((NZ, 2, NX, BLK, HW), BF),
            V((2, NX, NY, NZ, BLK, HW), BF),
            V(block, BF), V(block, BF), V(block, BF),
            V((KIN, BLK, BLK), BF), V((NCROSS, BLK, BLK), BF),
            V(block, BF), V(block, BF), V(block, BF), V(block, BF), V(block, BF),
            V((NCROSS + 1, BLK, F), F32), V((KIN + 1, BLK, F), F32),
            V((N_POS, 256), I32), V((4, 8, 256), I32), pltpu.SMEM((4, 8, 256), I32),
            V((NZ, 8, 128), I32), pltpu.SMEM((NZ, 8, 128), I32),
            V((NZ, 2, NX, NY, BLK, HW), BF),
            V((NZ, 2, NX, BLK, HW), BF),
            V((NZ, 2) + half, BF),
            V((4, 2) + half, BF), V((4, 2) + half, BF),
            V((N_DOM - 1,) + block, BF),
            V(block, BF), V(block, BF), V(block, BF), V(block, BF),
            V((F, F), F32), V((4, F // N_DOM, F), F32), V((8, 8, F), F32), V((NZ, 8, F), F32),
            dma((9,)), dma((NZ,)), dma((NZ,)),
            dma((2 * NZ,)), dma((2 * NZ,)),
            dma((NZ, 2, 2, 4)), dma((NZ, 2, 2, 4)),
            dma((NZ, 2)), dma((NZ, 2)),
            dma((NZ, 2, 2)),
            dma((3,)), dma((3,)),
            dma((NZ, 2, 4)), dma((NZ, 2, 4)), dma((NZ, 2)),
            dma((NZ, 2)), dma((NZ, 2)),
            dma((4, 2)), dma((4, 2)), dma((4, 2)), dma((4, 2)),
            dma((3,)), dma((3,)),
            dma((27,)), dma((27,)),
        ],
        compiler_params=pltpu.CompilerParams(
            collective_id=0, has_side_effects=True, vmem_limit_bytes=60 << 20),
        name="graph_layer",
    )(ints, ints, features, intra_vals, cross_vals, weight, cotangent)


def deliver_kernel(*refs):
    srcs, dsts, sems = refs[:3], refs[3:6], refs[6]
    copies = [pltpu.make_async_copy(a, b, sems.at[n]) for n, (a, b) in enumerate(zip(srcs, dsts))]
    for copy in copies:
        copy.start()
    for copy in copies:
        copy.wait()


def deliver(*arrays):
    vm = pl.BlockSpec(memory_space=pltpu.VMEM)
    hbm = pl.BlockSpec(memory_space=pl.ANY)
    return pl.pallas_call(
        deliver_kernel,
        out_shape=tuple(jax.ShapeDtypeStruct(a.shape, a.dtype) for a in arrays),
        in_specs=[vm] * 3,
        out_specs=(hbm,) * 3,
        scratch_shapes=[pltpu.SemaphoreType.DMA((3,))],
        name="deliver",
    )(*arrays)


def body(features, weight, cotangent, send_list, intra_rows, intra_src, intra_count, intra_vals,
         cross_rows, cross_cols, cross_vals):
    def placed(row, values):
        flat = values.reshape((-1, values.shape[-1]))
        return jnp.pad(flat, ((row, 16 - row - flat.shape[0]), (0, 128 - flat.shape[1])))

    ints = (placed(SEND, send_list.reshape(1, -1)) + placed(IROW, intra_rows) + placed(ISRC, intra_src)
            + placed(ICOUNT, intra_count) + placed(CROW, cross_rows) + placed(CCOL, cross_cols))
    act, input_grad, weight_grad = run(
        ints, features.reshape(RB, BLK, F), intra_vals[0, 0],
        cross_vals.reshape(NCROSS, BLK, BLK), weight, cotangent.reshape(RB, BLK, F))
    act, input_grad, weight_grad = deliver(act, input_grad, weight_grad)
    return act.reshape(RB * BLK, F), input_grad.reshape(RB * BLK, F), weight_grad


def solution(mesh):
    placed = (
        P(("dom", "dev"), None),
        P(),
        P(("dom", "dev"), None),
        P("dom", "dev", None, None),
        P("dom", "dev", None),
        P("dom", "dev", None),
        P("dom", "dev"),
        P("dom", "dev", None, None, None),
        P("dom", "dev", None, None),
        P("dom", "dev", None, None),
        P("dom", "dev", None, None, None, None),
    )
    return jax.shard_map(
        body,
        mesh=mesh,
        in_specs=placed,
        out_specs=(P(("dom", "dev"), None), P(("dom", "dev"), None), P()),
        check_vma=False,
    )
```

```python
import math

import jax
import jax.numpy as jnp
from jax import lax
from jax.experimental import pallas as pl
from jax.experimental.pallas import tpu as pltpu
from jax.sharding import PartitionSpec as P

MESH = pl.DeviceIdType.MESH
BF = jnp.bfloat16
F32 = jnp.float32
I32 = jnp.int32
NX, NY, NZ = 4, 2, 8
RB, BLK, F = 8, 128, 256
HW = F // 2
N_DOM = 4
KIN, KX = 32, 16
NCROSS = (N_DOM - 1) * KX
W_SCALE = 1.0 / math.sqrt(RB * BLK * NX * NY * NZ * N_DOM)
STRIP = 32
RELS = (0, -1, 1, -2, 2, -3, 3, 4)
SLOT = {rel: i for i, rel in enumerate(RELS)}
SEND, IROW, ISRC, ICOUNT, CROW, CCOL = 0, 1, 2, 3, 8, 11
POS_A, POS_B, POS_C, POS_D, N_POS = 0, 48, 80, 112, 160
KEY_A, KEY_B, KEY_C, KEY_D = 0, 32, 64, 160


def dev_of(x, yh, z):
    return x * 16 + yh * 8 + z


def remote(src, dst, send_sem, recv_sem, dom, dev):
    return pltpu.make_async_remote_copy(
        src_ref=src, dst_ref=dst, send_sem=send_sem, recv_sem=recv_sem,
        device_id=(dom, dev), device_id_type=MESH)


def order_tiles(ints, key_rows, found):
    count = ints[ICOUNT, 0]
    lane = lax.broadcasted_iota(I32, (8, 256), 1)
    keys_lane = jnp.full((8, 256), 9999, I32)

    def put(e, key, keys_lane):
        key_rows[pl.ds(e, 1), :] = jnp.full((1, 256), key, I32)
        return jnp.where(lane == e, key, keys_lane)

    def cross(e, keys_lane):
        o = e // KX
        keys_lane = put(POS_A + e, KEY_A + o * RB + ints[CROW + e // KX, e % KX], keys_lane)
        return put(POS_D + e, KEY_D + o * RB + ints[CCOL + e // KX, e % KX], keys_lane)

    def intra(k, keys_lane):
        keys_lane = put(POS_B + k, KEY_B + jnp.where(k < count, ints[IROW, k], RB), keys_lane)
        return put(POS_C + k, KEY_C + jnp.where(k < count, ints[ISRC, k], NX * NY * NZ), keys_lane)

    keys_lane = lax.fori_loop(0, NCROSS, cross, keys_lane)
    keys_lane = lax.fori_loop(0, KIN, intra, keys_lane)

    def step(t, sums):
        tile, le, eq, skey = sums
        base = pl.multiple_of(t * 8, 8)
        rows = key_rows[pl.ds(base, 8), :]
        sub = base + lax.broadcasted_iota(I32, (8, 256), 0)
        ahead = (keys_lane < rows) | ((keys_lane == rows) & (lane < sub))
        place = jnp.sum(jnp.where(ahead, 1, 0), axis=1, keepdims=True)
        here = place == lane
        tile = tile + jnp.where(here, sub, 0)
        skey = skey + jnp.where(here, rows, 0)
        le = le + jnp.where(rows <= lane, 1, 0)
        eq = eq + jnp.where(rows == lane, 1, 0)
        return tile, le, eq, skey

    zero = jnp.zeros((8, 256), I32)
    tile, le, eq, skey = lax.fori_loop(0, N_POS // 8, step, (zero, zero, zero, zero))
    for r, value in enumerate((tile, le, eq, skey)):
        found[r] = jnp.broadcast_to(jnp.sum(value, axis=0, keepdims=True), (8, 256))


def kernel(ints, ints_vm, feat_hbm, ivals_hbm, cvals_hbm, w, cot_hbm,
           act_hbm, out, wg,
           *scr):
    it = iter(scr)
    feat = next(it)
    own = (next(it), next(it))
    bufs = {0: own}
    for rel in RELS[1:]:
        bufs[rel] = (next(it), next(it))
    (stage, relay, pool, rem_sib, rem_far0, rem_far1, rem_sf, ivals, cvals, cot, act, agg, grad, back,
     runs_a, runs_b, key_rows, found, found_sm, tab_vm, tab_sm,
     xbuf, ybuf, part, rin, lin, csums, near, pair, far_in, far_got, wpart, wquarter, wplane, wline,
     loc, meta_s, meta_r, zs, zr, xs, xr, ys, yr, ls, ds, dr,
     bxs, bxr, bls, bys, byr, rs, rr, lts, ltr, bds, bdr, ws, wr) = it
    dom = lax.axis_index("dom")
    dev = lax.axis_index("dev")
    x, yh, z = dev // 16, (dev // 8) % 2, dev % 8
    yo = 1 - yh
    here = x * NY + yh

    def zdev(rel):
        return dev_of(x, yh, (z + rel + NZ) % NZ)

    def xdev(dx):
        return dev_of((x + dx) % NX, yh, z)

    plane = [(dx, dy) for dy in (0, 1) for dx in range(NX) if dx or dy]

    def pdev(dx, dy):
        return dev_of((x + dx) % NX, (yh + dy) % NY, z)

    ydev = dev_of(x, yo, z)
    sib = dom + 1 - 2 * (dom % 2)
    far = (dom + 2) % N_DOM
    sf = (sib + 2) % N_DOM
    doms = (sib, far, sf)

    def o_of(other):
        return (dom - other - 1 + 2 * N_DOM) % N_DOM

    loads = []

    def load(src, dst):
        copy = pltpu.make_async_copy(src, dst, loc.at[len(loads)])
        copy.start()
        loads.append(copy)
        return copy

    peers = ([(dom, zdev(rel)) for rel in RELS[1:]] + [(dom, pdev(dx, dy)) for dx, dy in plane]
             + [(d, dev) for d in doms] + [(far, ydev)])
    barrier = pltpu.get_barrier_semaphore()
    for d, e in peers:
        pl.semaphore_signal(barrier, inc=1, device_id=(d, e), device_id_type=MESH)
    to_half = [load(feat_hbm.at[:, :, pl.ds(h * HW, HW)], own[h]) for h in (0, 1)]
    to_half[0].wait()
    to_half[1].wait()
    to_feat = load(feat_hbm, feat)
    to_cvals = load(cvals_hbm, cvals)
    to_ivals = load(ivals_hbm, ivals)
    to_cot = load(cot_hbm, cot)
    pl.semaphore_wait(barrier, len(peers))

    live = []

    def go(copy):
        copy.start()
        live.append(copy)

    def zcopy(src_rel, dst_rel, h):
        s = SLOT[dst_rel] * 2 + h
        to = 1 if dst_rel < 0 or (dst_rel == 4 and h == 0) else -1
        return remote(bufs[src_rel][h], bufs[dst_rel][h], zs.at[s], zr.at[s], dom, zdev(to))

    def zarrived(rel, h):
        zcopy(0, rel, h).wait_recv()

    def meta(rel):
        i = SLOT[-rel] if rel != 4 else SLOT[4]
        return remote(ints_vm.at[pl.ds(0, 8)], tab_vm.at[i], meta_s.at[i], meta_r.at[i], dom, zdev(rel))

    rem_far = (rem_far0, rem_far1)
    halves = [pl.ds(h * HW, HW) for h in (0, 1)]

    def to_sib():
        return remote(feat, rem_sib, ds.at[0], dr.at[0], sib, dev)

    def to_far(h):
        return remote(own[h], rem_far[h], ds.at[1 + h], dr.at[1 + h], far, dev)

    def far_to_sib(h):
        return remote(rem_far[h], rem_sf.at[:, :, halves[h]], ds.at[3 + h], dr.at[3 + h], sib, dev)

    def meta_far():
        return remote(ints_vm.at[pl.ds(0, 8)], tab_vm.at[NZ], meta_s.at[NZ], meta_r.at[NZ], far, dev)

    def ycopy(rel, h):
        i = SLOT[rel]
        return remote(stage.at[i, h, 0], relay.at[i, h], ys.at[i, h], yr.at[i, h], dom, ydev)

    def serve(rel, h):
        i = SLOT[rel]
        buf = bufs[rel][h]
        zsrc = (z + rel + NZ) % NZ
        for g, y in ((0, yo), (1, yh)):
            for xx in range(NX):
                where = dev_of(xx, y, z)
                pick = ints[SEND, where] if rel == 0 else tab_sm[i, SEND, where]
                stage[i, h, g, xx] = buf[pick]
            if g == 0:
                go(ycopy(rel, h))
        for dx in (1, 2, 3):
            go(remote(stage.at[i, h, 1, (x + dx) % NX], pool.at[h, x, yh, zsrc],
                      xs.at[i, h, 0, dx], xr.at[i, h, 0, dx], dom, xdev(dx)))
        go(pltpu.make_async_copy(stage.at[i, h, 1, x], pool.at[h, x, yh, zsrc], ls.at[i, h, 0]))

    def pass_on(rel, h):
        i = SLOT[rel]
        zsrc = (z + rel + NZ) % NZ
        ycopy(rel, h).wait_recv()
        for dx in (1, 2, 3):
            go(remote(relay.at[i, h, (x + dx) % NX], pool.at[h, x, yo, zsrc],
                      xs.at[i, h, 1, dx], xr.at[i, h, 1, dx], dom, xdev(dx)))
        go(pltpu.make_async_copy(relay.at[i, h, x], pool.at[h, x, yo, zsrc], ls.at[i, h, 1]))

    for rel in RELS[1:]:
        go(meta(rel))
    go(meta_far())
    for h in (0, 1):
        go(zcopy(0, -1, h))
        go(zcopy(0, 1, 1 - h))
    serve(0, 0)
    serve(0, 1)
    go(to_far(0))
    go(to_far(1))
    to_feat.wait()
    go(to_sib())

    order_tiles(ints, key_rows, found)
    to_found = load(found, found_sm)
    runs_a[0] = jnp.zeros((BLK, F), F32)
    runs_b[0] = jnp.zeros((BLK, F), F32)

    for rel in RELS[1:]:
        meta(rel).wait_recv()
    meta_far().wait_recv()
    tab_vm[0] = ints_vm[:8]
    to_tab = load(tab_vm, tab_sm)
    to_found.wait()
    to_tab.wait()

    def tile_at(i):
        return found_sm[0, 0, i]

    def joined(i, before, product):
        same = (i > 0) & (found_sm[3, 0, i] == found_sm[3, 0, jnp.maximum(i - 1, 0)])
        return product + jnp.where(same, before, 0.0)

    def cross_forward(pick, o, half):
        def step(u4, carry):
            for u in range(4):
                i = o * KX + half * (KX // 2) + u4 * 4 + u
                e = tile_at(POS_A + i)
                product = jnp.dot(cvals[e], pick(ints[CCOL + e // KX, e % KX]), preferred_element_type=F32)
                runs_a[i + 1] = joined(POS_A + i, runs_a[i], product)
            return carry
        lax.fori_loop(0, KX // 8, step, 0)

    to_cvals.wait()
    items = [(s * j, h if s < 0 else 1 - h) for j in (1, 2, 3) for h in (0, 1) for s in (-1, 1)]
    items = [(0, 0), (0, 1)] + items + [(4, 0), (4, 1)]
    LAG = 3
    for n in range(2, len(items) + LAG):
        if n < len(items):
            rel, h = items[n]
            zarrived(rel, h)
            if rel != 4:
                nxt = rel - 1 if rel < 0 else rel + 1
                if nxt == -4 and h == 0:
                    go(zcopy(rel, 4, 0))
                elif nxt == 4 and h == 1:
                    go(zcopy(rel, 4, 1))
                elif abs(nxt) < 4:
                    go(zcopy(rel, nxt, h))
            serve(rel, h)
        if n - LAG >= 0:
            pass_on(*items[n - LAG])
        if n in (3, 5):
            h = (n - 3) // 2
            to_far(h).wait_recv()
            go(far_to_sib(h))
        if n == 4:
            to_sib().wait_recv()
        if n == 9:
            far_to_sib(0).wait_recv()
            far_to_sib(1).wait_recv()
        if n in (4, 5):
            cross_forward(lambda c: rem_sib[c], o_of(sib), n - 4)
        if n in (7, 8):
            cross_forward(lambda c: jnp.concatenate([rem_far0[c], rem_far1[c]], axis=1), o_of(far), n - 7)
        if n in (10, 11):
            cross_forward(lambda c: rem_sf[c], o_of(sf), n - 10)

    for rel, h in items:
        i = SLOT[rel]
        for g in (0, 1):
            for dx in (1, 2, 3):
                remote(relay.at[0, 0, 0], pool.at[0, 0, 0, 0], xs.at[i, h, g, dx], xr.at[i, h, g, dx],
                       dom, xdev(dx)).wait_recv()
    for copy in live:
        if copy.is_remote:
            copy.wait_send()
        else:
            copy.wait()
    live.clear()
    to_ivals.wait()
    to_cot.wait()

    def intra_forward(u4, carry):
        for u in range(4):
            i = u4 * 4 + u
            k = tile_at(POS_B + i) - POS_B
            src = ints[ISRC, k]
            sx, sy, sz = src // 16, (src // 8) % 2, src % 8
            picked = jnp.concatenate([pool[0, sx, sy, sz], pool[1, sx, sy, sz]], axis=1)
            product = jnp.dot(ivals[k], picked, preferred_element_type=F32)
            runs_b[i + 1] = joined(POS_B + i, runs_b[i], product)
        return carry
    lax.fori_loop(0, KIN // 4, intra_forward, 0)

    def run_of(runs, key, first):
        last = jnp.maximum(found_sm[1, 0, key] - first, 0)
        return jnp.where(found_sm[2, 0, key] > 0, runs[last], 0.0)

    def dense(r, carry):
        total = run_of(runs_b, KEY_B + r, POS_B)
        for o in range(N_DOM - 1):
            total = total + run_of(runs_a, KEY_A + o * RB + r, POS_A)
        agg_r = total.astype(BF)
        agg[r] = agg_r
        pre = jnp.dot(agg_r, w[...], preferred_element_type=F32)
        sig = jax.nn.sigmoid(pre)
        act[r] = (pre * sig).astype(BF)
        grad_r = (cot[r].astype(F32) * sig * (1.0 + pre * (1.0 - sig))).astype(BF)
        grad[r] = grad_r
        back[r] = lax.dot_general(
            grad_r, w[...], (((1,), (1,)), ((), ())), preferred_element_type=F32).astype(BF)
        return carry
    lax.fori_loop(0, RB, dense, 0)

    turned = (((0,), (0,)), ((), ()))

    def intra_back(u4, carry):
        for u in range(4):
            i = u4 * 4 + u
            k = tile_at(POS_C + i) - POS_C
            product = lax.dot_general(ivals[k], back[ints[IROW, k]], turned, preferred_element_type=F32)
            runs_b[i + 1] = joined(POS_C + i, runs_b[i], product)
        return carry
    lax.fori_loop(0, KIN // 4, intra_back, 0)

    def fill(rel):
        zdst = (z + rel + NZ) % NZ

        def one(c, carry):
            total = run_of(runs_b, KEY_C + (c // NY) * 16 + (c % NY) * 8 + zdst, POS_C).astype(BF)
            pool[0, c // NY, c % NY, zdst] = total[:, :HW]
            pool[1, c // NY, c % NY, zdst] = total[:, HW:]
            return carry
        lax.fori_loop(0, NX * NY, one, 0)

    def bxcopy(rel, h, dx):
        i = SLOT[rel]
        zdst = (z + rel + NZ) % NZ
        return remote(pool.at[h, (x + dx) % NX, :, zdst], xbuf.at[i, h, dx], bxs.at[i, h, dx],
                      bxr.at[i, h, dx], dom, xdev(dx))

    def bown(rel, h):
        i = SLOT[rel]
        zdst = (z + rel + NZ) % NZ
        return pltpu.make_async_copy(pool.at[h, x, :, zdst], xbuf.at[i, h, 0], bls.at[i, h])

    def xsend(rel, h):
        for dx in (1, 2, 3):
            go(bxcopy(rel, h, dx))
        bown(rel, h).start()

    def bycopy(rel, h):
        i = SLOT[rel]
        return remote(xbuf.at[i, h, :, yo], ybuf.at[i, h], bys.at[i, h], byr.at[i, h],
                      far if rel == 0 else dom, ydev)

    def ysend(rel, h):
        for dx in (1, 2, 3):
            bxcopy(rel, h, dx).wait_recv()
        bown(rel, h).wait()
        go(bycopy(rel, h))

    def rcopy(src_rel, j, h):
        return remote(part.at[SLOT[src_rel], h], rin.at[j, h], rs.at[j, h], rr.at[j, h], dom, zdev(1))

    def lcopy(src_rel, j, h):
        return remote(part.at[SLOT[src_rel], h], lin.at[j, h], lts.at[j, h], ltr.at[j, h], dom, zdev(-1))

    def combine(groups, h, extra, store):
        picks = []
        for g, (buf, tab, y) in enumerate(groups):
            for dx in range(NX):
                pick = tab_sm[tab, SEND, dev_of((x - dx + NX) % NX, y, z)]
                picks.append((buf, dx, [jnp.where(pick == b, 1.0, 0.0).astype(F32) for b in range(RB)]))

        def strip(s, carry):
            rows = pl.ds(pl.multiple_of(s * STRIP, STRIP), STRIP)
            totals = [None] * RB
            for buf, dx, on in picks:
                got = buf[dx, rows].astype(F32)
                for b in range(RB):
                    term = got * on[b]
                    totals[b] = term if totals[b] is None else totals[b] + term
            for b in range(RB):
                total = totals[b]
                for ref in extra:
                    total = total + ref[b, rows].astype(F32)
                store(b, rows, total.astype(BF))
            return carry
        lax.fori_loop(0, BLK // STRIP, strip, 0)

    def own_half(rel, h):
        return (xbuf.at[SLOT[rel], h, :, yh], SLOT[rel], yh)

    def other_half(rel, h):
        return (ybuf.at[SLOT[rel], h], SLOT[rel], yo)

    def sum_chunk(rel, h, extra):
        bycopy(rel, h).wait_recv()
        combine([own_half(rel, h), other_half(rel, h)], h, extra, into_part(rel, h))

    def into_part(rel, h):
        def store(b, rows, value):
            part[SLOT[rel], h, b, rows] = value
        return store

    def cross_back(other):
        o = o_of(other)

        def step(u4, carry):
            for u in range(4):
                i = o * KX + u4 * 4 + u
                e = tile_at(POS_D + i) - POS_D
                product = lax.dot_general(cvals[e], back[ints[CROW + e // KX, e % KX]], turned, preferred_element_type=F32)
                runs_a[i + 1] = joined(POS_D + i, runs_a[i], product)
            return carry
        lax.fori_loop(0, KX // 4, step, 0)

        def one(b, carry):
            csums[o, b] = run_of(runs_a, KEY_D + o * RB + b, POS_D).astype(BF)
            return carry
        lax.fori_loop(0, RB, one, 0)

    wrows = F // N_DOM
    first = dom * wrows + here * 8

    def w_dom(n):
        return remote(wpart.at[pl.ds(doms[n] * wrows, wrows)], wquarter.at[n], ws.at[n], wr.at[n], doms[n], dev)

    def w_plane(n):
        dx, dy = plane[n]
        there = ((x + dx) % NX) * NY + (yh + dy) % NY
        return remote(wquarter.at[3, pl.ds(there * 8, 8)], wplane.at[n], ws.at[3 + n], wr.at[3 + n],
                      dom, pdev(dx, dy))

    def w_line(n):
        return remote(wplane.at[7], wline.at[z], ws.at[10 + n], wr.at[10 + n], dom, zdev(RELS[1 + n]))

    def w_plane_back(n):
        dx, dy = plane[n]
        rows = pl.ds(first, 8)
        return remote(wg.at[rows], wg.at[rows], ws.at[17 + n], wr.at[17 + n], dom, pdev(dx, dy))

    def w_dom_back(n):
        rows = pl.ds(dom * wrows, wrows)
        return remote(wg.at[rows], wg.at[rows], ws.at[24 + n], wr.at[24 + n], doms[n], dev)

    def w_step(step):
        if step == 0:
            wpart[...] = jnp.zeros_like(wpart)

            def add(r, carry):
                wpart[...] += lax.dot_general(agg[r], grad[r], turned, preferred_element_type=F32)
                return carry
            lax.fori_loop(0, RB, add, 0)
            for n in range(3):
                go(w_dom(n))
        if step == 1:
            for n in range(3):
                w_dom(n).wait_recv()
            wquarter[3] = (wpart[pl.ds(dom * wrows, wrows)] + wquarter[0]) + (wquarter[1] + wquarter[2])
            for n in range(7):
                go(w_plane(n))
        if step == 2:
            for n in range(7):
                w_plane(n).wait_recv()
            total = wquarter[3, pl.ds(here * 8, 8)]
            for n in range(7):
                total = total + wplane[n]
            wplane[7] = total
            wline[z] = total
            for n in range(7):
                go(w_line(n))
        if step == 3:
            for n in range(7):
                w_line(n).wait_recv()
            total = wline[0]
            for n in range(1, NZ):
                total = total + wline[n]
            wg[pl.ds(first, 8)] = total * W_SCALE
            for n in range(7):
                go(w_plane_back(n))
        if step == 4:
            for n in range(7):
                w_plane_back(n).wait_recv()
            for n in range(3):
                go(w_dom_back(n))
        if step == 5:
            for n in range(3):
                w_dom_back(n).wait_recv()

    def bd(n, h=0):
        if n == 0:
            return remote(csums.at[o_of(sf)], pair, bds.at[0], bdr.at[0], sib, dev)
        if n == 1:
            return remote(csums.at[o_of(sib)], near, bds.at[1], bdr.at[1], sib, dev)
        return remote(far_in.at[:, :, halves[h]], far_got.at[:, :, halves[h]], bds.at[2 + h], bdr.at[2 + h],
                      far, dev)

    def sum_far(h):
        bycopy(0, h).wait_recv()

        def store(b, rows, value):
            far_in[b, rows, halves[h]] = value
        combine([(ybuf.at[0, h], NZ, yo)], h,
                [pair.at[:, :, halves[h]], csums.at[o_of(far), :, :, halves[h]]], store)

    turns = [(4, 0), (4, 1)] + [(s * j, h if s > 0 else 1 - h)
                                for j in (3, 2, 1) for h in (0, 1) for s in (1, -1)] + [(0, 0), (0, 1)]
    n_turns = len(turns)
    queue = turns[:6] + [(0, 0), (0, 1)] + turns[6:14]
    filled = set()
    sent = {"x": 0, "y": 0}

    def xgo(upto):
        while sent["x"] < min(upto, n_turns):
            rel, h = queue[sent["x"]]
            if rel not in filled:
                filled.add(rel)
                fill(rel)
            xsend(rel, h)
            sent["x"] += 1

    def ygo(upto):
        while sent["y"] < min(upto, n_turns):
            ysend(*queue[sent["y"]])
            sent["y"] += 1

    def finish(n):
        rel, h = turns[n]
        if rel == 4:
            sum_chunk(4, h, [])
            go(rcopy(4, 3, 0) if h == 0 else lcopy(4, 3, 1))
        elif rel > 0:
            extra = []
            if rel < 3 or h == 0:
                rcopy(4, rel, h).wait_recv()
                extra = [rin.at[rel, h]]
            sum_chunk(rel, h, extra)
            go(rcopy(rel, rel - 1, h))
        elif rel < 0:
            extra = []
            if rel > -3 or h == 1:
                lcopy(4, -rel, h).wait_recv()
                extra = [lin.at[-rel, h]]
            sum_chunk(rel, h, extra)
            go(lcopy(rel, -rel - 1, h))
        else:
            rcopy(4, 0, h).wait_recv()
            lcopy(4, 0, h).wait_recv()
            cols = pl.ds(h * HW, HW)

            def store(b, rows, value):
                out[b, rows, cols] = value
            combine([own_half(0, h)], h, [rin.at[0, h], lin.at[0, h], near.at[:, :, cols], far_got.at[:, :, cols]], store)

    xgo(6)
    to_act = load(act, act_hbm)
    w_step(0)
    ygo(1)
    cross_back(sf)
    go(bd(0))
    ygo(2)
    cross_back(far)
    xgo(8)
    ygo(3)
    for n in range(n_turns):
        lead = 4 if n < 3 else 5 if n < 5 else 6
        xgo(n + lead + 4)
        ygo(n + lead)
        if n == 8:
            bd(0).wait_recv()
        if n in (8, 9):
            sum_far(n - 8)
        if n in (10, 11):
            go(bd(2, n - 10))
        if n == n_turns - 2:
            bd(1).wait_recv()
        if n >= n_turns - 2:
            bd(2, n - n_turns + 2).wait_recv()
        finish(n)
        if n == 1:
            cross_back(sib)
            go(bd(1))
        if n in (3, 5, 7, 9):
            w_step((n - 1) // 2)
    w_step(5)
    for copy in live:
        copy.wait_send()
    to_act.wait()


def run(ints, features, intra_vals, cross_vals, weight, cotangent):
    vm = pl.BlockSpec(memory_space=pltpu.VMEM)
    sm = pl.BlockSpec(memory_space=pltpu.SMEM)
    hbm = pl.BlockSpec(memory_space=pl.ANY)
    dma = pltpu.SemaphoreType.DMA
    block = (RB, BLK, F)
    half = (RB, BLK, HW)
    V = pltpu.VMEM
    return pl.pallas_call(
        kernel,
        out_shape=(
            jax.ShapeDtypeStruct(block, BF),
            jax.ShapeDtypeStruct(block, BF),
            jax.ShapeDtypeStruct((F, F), F32),
        ),
        in_specs=[sm, vm, hbm, hbm, hbm, vm, hbm],
        out_specs=(hbm, vm, vm),
        scratch_shapes=[V(block, BF)] + [V(half, BF)] * 16 + [
            V((NZ, 2, NY, NX, BLK, HW), BF),
            V((NZ, 2, NX, BLK, HW), BF),
            V((2, NX, NY, NZ, BLK, HW), BF),
            V(block, BF), V(half, BF), V(half, BF), V(block, BF),
            V((KIN, BLK, BLK), BF), V((NCROSS, BLK, BLK), BF),
            V(block, BF), V(block, BF), V(block, BF), V(block, BF), V(block, BF),
            V((NCROSS + 1, BLK, F), F32), V((KIN + 1, BLK, F), F32),
            V((N_POS, 256), I32), V((4, 8, 256), I32), pltpu.SMEM((4, 8, 256), I32),
            V((NZ + 1, 8, 128), I32), pltpu.SMEM((NZ + 1, 8, 128), I32),
            V((NZ, 2, NX, NY, BLK, HW), BF),
            V((NZ, 2, NX, BLK, HW), BF),
            V((NZ, 2) + half, BF),
            V((4, 2) + half, BF), V((4, 2) + half, BF),
            V((N_DOM - 1,) + block, BF),
            V(block, BF), V(block, BF), V(block, BF), V(block, BF),
            V((F, F), F32), V((4, F // N_DOM, F), F32), V((8, 8, F), F32), V((NZ, 8, F), F32),
            dma((9,)), dma((NZ + 1,)), dma((NZ + 1,)),
            dma((2 * NZ,)), dma((2 * NZ,)),
            dma((NZ, 2, 2, 4)), dma((NZ, 2, 2, 4)),
            dma((NZ, 2)), dma((NZ, 2)),
            dma((NZ, 2, 2)),
            dma((5,)), dma((5,)),
            dma((NZ, 2, 4)), dma((NZ, 2, 4)), dma((NZ, 2)),
            dma((NZ, 2)), dma((NZ, 2)),
            dma((4, 2)), dma((4, 2)), dma((4, 2)), dma((4, 2)),
            dma((4,)), dma((4,)),
            dma((27,)), dma((27,)),
        ],
        compiler_params=pltpu.CompilerParams(
            collective_id=0, has_side_effects=True, vmem_limit_bytes=60 << 20),
        name="graph_layer",
    )(ints, ints, features, intra_vals, cross_vals, weight, cotangent)


def deliver_kernel(*refs):
    srcs, dsts, sems = refs[:3], refs[3:6], refs[6]
    copies = [pltpu.make_async_copy(a, b, sems.at[n]) for n, (a, b) in enumerate(zip(srcs, dsts))]
    for copy in copies:
        copy.start()
    for copy in copies:
        copy.wait()


def deliver(*arrays):
    vm = pl.BlockSpec(memory_space=pltpu.VMEM)
    hbm = pl.BlockSpec(memory_space=pl.ANY)
    return pl.pallas_call(
        deliver_kernel,
        out_shape=tuple(jax.ShapeDtypeStruct(a.shape, a.dtype) for a in arrays),
        in_specs=[vm] * 3,
        out_specs=(hbm,) * 3,
        scratch_shapes=[pltpu.SemaphoreType.DMA((3,))],
        name="deliver",
    )(*arrays)


def body(features, weight, cotangent, send_list, intra_rows, intra_src, intra_count, intra_vals,
         cross_rows, cross_cols, cross_vals):
    def placed(row, values):
        flat = values.reshape((-1, values.shape[-1]))
        return jnp.pad(flat, ((row, 16 - row - flat.shape[0]), (0, 128 - flat.shape[1])))

    ints = (placed(SEND, send_list.reshape(1, -1)) + placed(IROW, intra_rows) + placed(ISRC, intra_src)
            + placed(ICOUNT, intra_count) + placed(CROW, cross_rows) + placed(CCOL, cross_cols))
    act, input_grad, weight_grad = run(
        ints, features.reshape(RB, BLK, F), intra_vals[0, 0],
        cross_vals.reshape(NCROSS, BLK, BLK), weight, cotangent.reshape(RB, BLK, F))
    act, input_grad, weight_grad = deliver(act, input_grad, weight_grad)
    return act.reshape(RB * BLK, F), input_grad.reshape(RB * BLK, F), weight_grad


def solution(mesh):
    placed = (
        P(("dom", "dev"), None),
        P(),
        P(("dom", "dev"), None),
        P("dom", "dev", None, None),
        P("dom", "dev", None),
        P("dom", "dev", None),
        P("dom", "dev"),
        P("dom", "dev", None, None, None),
        P("dom", "dev", None, None),
        P("dom", "dev", None, None),
        P("dom", "dev", None, None, None, None),
    )
    return jax.shard_map(
        body,
        mesh=mesh,
        in_specs=placed,
        out_specs=(P(("dom", "dev"), None), P(("dom", "dev"), None), P()),
        check_vma=False,
    )
```

```python
import math

import jax
import jax.numpy as jnp
from jax import lax
from jax.experimental import pallas as pl
from jax.experimental.pallas import tpu as pltpu
from jax.sharding import PartitionSpec as P

MESH = pl.DeviceIdType.MESH
BF = jnp.bfloat16
F32 = jnp.float32
I32 = jnp.int32
NX, NY, NZ = 4, 2, 8
RB, BLK, F = 8, 128, 256
HW = F // 2
N_DOM = 4
KIN, KX = 32, 16
NCROSS = (N_DOM - 1) * KX
W_SCALE = 1.0 / math.sqrt(RB * BLK * NX * NY * NZ * N_DOM)
STRIP = 32
RELS = (0, -1, 1, -2, 2, -3, 3, 4)
SLOT = {rel: i for i, rel in enumerate(RELS)}
SEND, IROW, ISRC, ICOUNT, CROW, CCOL = 0, 1, 2, 3, 8, 11
POS_A, POS_B, POS_C, POS_D, N_POS = 0, 48, 80, 112, 160
KEY_A, KEY_B, KEY_C, KEY_D = 0, 32, 64, 160


def dev_of(x, yh, z):
    return x * 16 + yh * 8 + z


def remote(src, dst, send_sem, recv_sem, dom, dev):
    return pltpu.make_async_remote_copy(
        src_ref=src, dst_ref=dst, send_sem=send_sem, recv_sem=recv_sem,
        device_id=(dom, dev), device_id_type=MESH)


def order_tiles(ints, key_rows, found):
    count = ints[ICOUNT, 0]
    lane = lax.broadcasted_iota(I32, (8, 256), 1)
    keys_lane = jnp.full((8, 256), 9999, I32)

    def put(e, key, keys_lane):
        key_rows[pl.ds(e, 1), :] = jnp.full((1, 256), key, I32)
        return jnp.where(lane == e, key, keys_lane)

    def cross(e, keys_lane):
        o = e // KX
        keys_lane = put(POS_A + e, KEY_A + o * RB + ints[CROW + e // KX, e % KX], keys_lane)
        return put(POS_D + e, KEY_D + o * RB + ints[CCOL + e // KX, e % KX], keys_lane)

    def intra(k, keys_lane):
        keys_lane = put(POS_B + k, KEY_B + jnp.where(k < count, ints[IROW, k], RB), keys_lane)
        return put(POS_C + k, KEY_C + jnp.where(k < count, ints[ISRC, k], NX * NY * NZ), keys_lane)

    keys_lane = lax.fori_loop(0, NCROSS, cross, keys_lane)
    keys_lane = lax.fori_loop(0, KIN, intra, keys_lane)

    def step(t, sums):
        tile, le, eq, skey = sums
        base = pl.multiple_of(t * 8, 8)
        rows = key_rows[pl.ds(base, 8), :]
        sub = base + lax.broadcasted_iota(I32, (8, 256), 0)
        ahead = (keys_lane < rows) | ((keys_lane == rows) & (lane < sub))
        place = jnp.sum(jnp.where(ahead, 1, 0), axis=1, keepdims=True)
        here = place == lane
        tile = tile + jnp.where(here, sub, 0)
        skey = skey + jnp.where(here, rows, 0)
        le = le + jnp.where(rows <= lane, 1, 0)
        eq = eq + jnp.where(rows == lane, 1, 0)
        return tile, le, eq, skey

    zero = jnp.zeros((8, 256), I32)
    tile, le, eq, skey = lax.fori_loop(0, N_POS // 8, step, (zero, zero, zero, zero))
    for r, value in enumerate((tile, le, eq, skey)):
        found[r] = jnp.broadcast_to(jnp.sum(value, axis=0, keepdims=True), (8, 256))


def kernel(ints, ints_vm, feat_hbm, ivals_hbm, cvals_hbm, w, cot_hbm,
           act_hbm, out, wg,
           *scr):
    it = iter(scr)
    feat = next(it)
    own = (next(it), next(it))
    bufs = {0: own}
    for rel in RELS[1:]:
        bufs[rel] = (next(it), next(it))
    (stage, relay, pool, rem_sib, rem_far0, rem_far1, rem_sf, ivals, cvals, cot, act, agg, grad, back,
     runs_a, runs_b, key_rows, found, found_sm, tab_vm, tab_sm,
     xbuf, ybuf, part, rin, lin, csums, near, pair, far_in, far_got, wpart, wquarter, wplane, wline,
     loc, meta_s, meta_r, zs, zr, xs, xr, ys, yr, ls, ds, dr,
     bxs, bxr, bls, bys, byr, rs, rr, lts, ltr, bds, bdr, ws, wr) = it
    dom = lax.axis_index("dom")
    dev = lax.axis_index("dev")
    x, yh, z = dev // 16, (dev // 8) % 2, dev % 8
    yo = 1 - yh
    here = x * NY + yh

    def zdev(rel):
        return dev_of(x, yh, (z + rel + NZ) % NZ)

    def xdev(dx):
        return dev_of((x + dx) % NX, yh, z)

    plane = [(dx, dy) for dy in (0, 1) for dx in range(NX) if dx or dy]

    def pdev(dx, dy):
        return dev_of((x + dx) % NX, (yh + dy) % NY, z)

    ydev = dev_of(x, yo, z)
    sib = dom + 1 - 2 * (dom % 2)
    far = (dom + 2) % N_DOM
    sf = (sib + 2) % N_DOM
    doms = (sib, far, sf)

    def o_of(other):
        return (dom - other - 1 + 2 * N_DOM) % N_DOM

    loads = []

    def load(src, dst):
        copy = pltpu.make_async_copy(src, dst, loc.at[len(loads)])
        copy.start()
        loads.append(copy)
        return copy

    peers = ([(dom, zdev(rel)) for rel in RELS[1:]] + [(dom, pdev(dx, dy)) for dx, dy in plane]
             + [(d, dev) for d in doms] + [(far, ydev)])
    barrier = pltpu.get_barrier_semaphore()
    for d, e in peers:
        pl.semaphore_signal(barrier, inc=1, device_id=(d, e), device_id_type=MESH)
    to_half = [load(feat_hbm.at[:, :, pl.ds(h * HW, HW)], own[h]) for h in (0, 1)]
    to_half[0].wait()
    to_half[1].wait()
    to_feat = load(feat_hbm, feat)
    to_cvals = load(cvals_hbm, cvals)
    to_ivals = load(ivals_hbm, ivals)
    to_cot = load(cot_hbm, cot)
    pl.semaphore_wait(barrier, len(peers))

    live = []

    def go(copy):
        copy.start()
        live.append(copy)

    def zcopy(src_rel, dst_rel, h):
        s = SLOT[dst_rel] * 2 + h
        to = 1 if dst_rel < 0 or (dst_rel == 4 and h == 0) else -1
        return remote(bufs[src_rel][h], bufs[dst_rel][h], zs.at[s], zr.at[s], dom, zdev(to))

    def zarrived(rel, h):
        zcopy(0, rel, h).wait_recv()

    def meta(rel):
        i = SLOT[-rel] if rel != 4 else SLOT[4]
        return remote(ints_vm.at[pl.ds(0, 8)], tab_vm.at[i], meta_s.at[i], meta_r.at[i], dom, zdev(rel))

    rem_far = (rem_far0, rem_far1)
    halves = [pl.ds(h * HW, HW) for h in (0, 1)]

    def to_sib():
        return remote(feat, rem_sib, ds.at[0], dr.at[0], sib, dev)

    def to_far(h):
        return remote(own[h], rem_far[h], ds.at[1 + h], dr.at[1 + h], far, dev)

    def far_to_sib(h):
        return remote(rem_far[h], rem_sf.at[:, :, halves[h]], ds.at[3 + h], dr.at[3 + h], sib, dev)

    def meta_far():
        return remote(ints_vm.at[pl.ds(0, 8)], tab_vm.at[NZ], meta_s.at[NZ], meta_r.at[NZ], far, dev)

    def ycopy(rel, h):
        i = SLOT[rel]
        return remote(stage.at[i, h, 0], relay.at[i, h], ys.at[i, h], yr.at[i, h], dom, ydev)

    def serve(rel, h):
        i = SLOT[rel]
        buf = bufs[rel][h]
        zsrc = (z + rel + NZ) % NZ
        for g, y in ((0, yo), (1, yh)):
            for xx in range(NX):
                where = dev_of(xx, y, z)
                pick = ints[SEND, where] if rel == 0 else tab_sm[i, SEND, where]
                stage[i, h, g, xx] = buf[pick]
            if g == 0:
                go(ycopy(rel, h))
        for dx in (1, 2, 3):
            go(remote(stage.at[i, h, 1, (x + dx) % NX], pool.at[h, x, yh, zsrc],
                      xs.at[i, h, 0, dx], xr.at[i, h, 0, dx], dom, xdev(dx)))
        go(pltpu.make_async_copy(stage.at[i, h, 1, x], pool.at[h, x, yh, zsrc], ls.at[i, h, 0]))

    def pass_on(rel, h):
        i = SLOT[rel]
        zsrc = (z + rel + NZ) % NZ
        ycopy(rel, h).wait_recv()
        for dx in (1, 2, 3):
            go(remote(relay.at[i, h, (x + dx) % NX], pool.at[h, x, yo, zsrc],
                      xs.at[i, h, 1, dx], xr.at[i, h, 1, dx], dom, xdev(dx)))
        go(pltpu.make_async_copy(relay.at[i, h, x], pool.at[h, x, yo, zsrc], ls.at[i, h, 1]))

    for rel in RELS[1:]:
        go(meta(rel))
    go(meta_far())
    for h in (0, 1):
        go(zcopy(0, -1, h))
        go(zcopy(0, 1, 1 - h))
    serve(0, 0)
    serve(0, 1)
    go(to_far(0))
    go(to_far(1))
    to_feat.wait()
    go(to_sib())

    order_tiles(ints, key_rows, found)
    to_found = load(found, found_sm)
    runs_a[0] = jnp.zeros((BLK, F), F32)
    runs_b[0] = jnp.zeros((BLK, F), F32)

    for rel in RELS[1:]:
        meta(rel).wait_recv()
    meta_far().wait_recv()
    tab_vm[0] = ints_vm[:8]
    to_tab = load(tab_vm, tab_sm)
    to_found.wait()
    to_tab.wait()

    def tile_at(i):
        return found_sm[0, 0, i]

    def joined(i, before, product):
        same = (i > 0) & (found_sm[3, 0, i] == found_sm[3, 0, jnp.maximum(i - 1, 0)])
        return product + jnp.where(same, before, 0.0)

    def cross_forward(pick, o, half):
        def step(u4, carry):
            for u in range(4):
                i = o * KX + half * (KX // 2) + u4 * 4 + u
                e = tile_at(POS_A + i)
                product = jnp.dot(cvals[e], pick(ints[CCOL + e // KX, e % KX]), preferred_element_type=F32)
                runs_a[i + 1] = joined(POS_A + i, runs_a[i], product)
            return carry
        lax.fori_loop(0, KX // 8, step, 0)

    to_cvals.wait()
    items = [(s * j, h if s < 0 else 1 - h) for j in (1, 2, 3) for h in (0, 1) for s in (-1, 1)]
    items = [(0, 0), (0, 1)] + items + [(4, 0), (4, 1)]
    LAG = 3
    for n in range(2, len(items) + LAG):
        if n < len(items):
            rel, h = items[n]
            zarrived(rel, h)
            if rel != 4:
                nxt = rel - 1 if rel < 0 else rel + 1
                if nxt == -4 and h == 0:
                    go(zcopy(rel, 4, 0))
                elif nxt == 4 and h == 1:
                    go(zcopy(rel, 4, 1))
                elif abs(nxt) < 4:
                    go(zcopy(rel, nxt, h))
            serve(rel, h)
        if n - LAG >= 0:
            pass_on(*items[n - LAG])
        if n in (3, 5):
            h = (n - 3) // 2
            to_far(h).wait_recv()
            go(far_to_sib(h))
        if n == 4:
            to_sib().wait_recv()
        if n == 9:
            far_to_sib(0).wait_recv()
            far_to_sib(1).wait_recv()
        if n in (4, 5):
            cross_forward(lambda c: rem_sib[c], o_of(sib), n - 4)
        if n in (7, 8):
            cross_forward(lambda c: jnp.concatenate([rem_far0[c], rem_far1[c]], axis=1), o_of(far), n - 7)
        if n in (10, 11):
            cross_forward(lambda c: rem_sf[c], o_of(sf), n - 10)

    for rel, h in items:
        i = SLOT[rel]
        for g in (0, 1):
            for dx in (1, 2, 3):
                remote(relay.at[0, 0, 0], pool.at[0, 0, 0, 0], xs.at[i, h, g, dx], xr.at[i, h, g, dx],
                       dom, xdev(dx)).wait_recv()
    for copy in live:
        if copy.is_remote:
            copy.wait_send()
        else:
            copy.wait()
    live.clear()
    to_ivals.wait()
    to_cot.wait()

    def intra_forward(u4, carry):
        for u in range(4):
            i = u4 * 4 + u
            k = tile_at(POS_B + i) - POS_B
            src = ints[ISRC, k]
            sx, sy, sz = src // 16, (src // 8) % 2, src % 8
            picked = jnp.concatenate([pool[0, sx, sy, sz], pool[1, sx, sy, sz]], axis=1)
            product = jnp.dot(ivals[k], picked, preferred_element_type=F32)
            runs_b[i + 1] = joined(POS_B + i, runs_b[i], product)
        return carry
    lax.fori_loop(0, KIN // 4, intra_forward, 0)

    def run_of(runs, key, first):
        last = jnp.maximum(found_sm[1, 0, key] - first, 0)
        return jnp.where(found_sm[2, 0, key] > 0, runs[last], 0.0)

    def dense(r, carry):
        total = run_of(runs_b, KEY_B + r, POS_B)
        for o in range(N_DOM - 1):
            total = total + run_of(runs_a, KEY_A + o * RB + r, POS_A)
        agg_r = total.astype(BF)
        agg[r] = agg_r
        pre = jnp.dot(agg_r, w[...], preferred_element_type=F32)
        sig = jax.nn.sigmoid(pre)
        act[r] = (pre * sig).astype(BF)
        grad_r = (cot[r].astype(F32) * sig * (1.0 + pre * (1.0 - sig))).astype(BF)
        grad[r] = grad_r
        back[r] = lax.dot_general(
            grad_r, w[...], (((1,), (1,)), ((), ())), preferred_element_type=F32).astype(BF)
        return carry
    lax.fori_loop(0, RB, dense, 0)

    turned = (((0,), (0,)), ((), ()))

    def intra_back(u4, carry):
        for u in range(4):
            i = u4 * 4 + u
            k = tile_at(POS_C + i) - POS_C
            product = lax.dot_general(ivals[k], back[ints[IROW, k]], turned, preferred_element_type=F32)
            runs_b[i + 1] = joined(POS_C + i, runs_b[i], product)
        return carry
    lax.fori_loop(0, KIN // 4, intra_back, 0)

    def fill(rel):
        zdst = (z + rel + NZ) % NZ

        def one(c, carry):
            total = run_of(runs_b, KEY_C + (c // NY) * 16 + (c % NY) * 8 + zdst, POS_C).astype(BF)
            pool[0, c // NY, c % NY, zdst] = total[:, :HW]
            pool[1, c // NY, c % NY, zdst] = total[:, HW:]
            return carry
        lax.fori_loop(0, NX * NY, one, 0)

    def bxcopy(rel, h, dx):
        i = SLOT[rel]
        zdst = (z + rel + NZ) % NZ
        return remote(pool.at[h, (x + dx) % NX, :, zdst], xbuf.at[i, h, dx], bxs.at[i, h, dx],
                      bxr.at[i, h, dx], dom, xdev(dx))

    def bown(rel, h):
        i = SLOT[rel]
        zdst = (z + rel + NZ) % NZ
        return pltpu.make_async_copy(pool.at[h, x, :, zdst], xbuf.at[i, h, 0], bls.at[i, h])

    def xsend(rel, h):
        for dx in (1, 2, 3):
            go(bxcopy(rel, h, dx))
        bown(rel, h).start()

    def bycopy(rel, h):
        i = SLOT[rel]
        return remote(xbuf.at[i, h, :, yo], ybuf.at[i, h], bys.at[i, h], byr.at[i, h],
                      far if rel == 0 else dom, ydev)

    def ysend(rel, h):
        for dx in (1, 2, 3):
            bxcopy(rel, h, dx).wait_recv()
        bown(rel, h).wait()
        go(bycopy(rel, h))

    def rcopy(src_rel, j, h):
        return remote(part.at[SLOT[src_rel], h], rin.at[j, h], rs.at[j, h], rr.at[j, h], dom, zdev(1))

    def lcopy(src_rel, j, h):
        return remote(part.at[SLOT[src_rel], h], lin.at[j, h], lts.at[j, h], ltr.at[j, h], dom, zdev(-1))

    def combine(groups, h, extra, store):
        picks = []
        for g, (buf, tab, y) in enumerate(groups):
            for dx in range(NX):
                pick = tab_sm[tab, SEND, dev_of((x - dx + NX) % NX, y, z)]
                picks.append((buf, dx, [jnp.where(pick == b, 1.0, 0.0).astype(F32) for b in range(RB)]))

        def strip(s, carry):
            rows = pl.ds(pl.multiple_of(s * STRIP, STRIP), STRIP)
            totals = [None] * RB
            for buf, dx, on in picks:
                got = buf[dx, rows].astype(F32)
                for b in range(RB):
                    term = got * on[b]
                    totals[b] = term if totals[b] is None else totals[b] + term
            for b in range(RB):
                total = totals[b]
                for ref in extra:
                    total = total + ref[b, rows].astype(F32)
                store(b, rows, total.astype(BF))
            return carry
        lax.fori_loop(0, BLK // STRIP, strip, 0)

    def own_half(rel, h):
        return (xbuf.at[SLOT[rel], h, :, yh], SLOT[rel], yh)

    def other_half(rel, h):
        return (ybuf.at[SLOT[rel], h], SLOT[rel], yo)

    def sum_chunk(rel, h, extra):
        bycopy(rel, h).wait_recv()
        combine([own_half(rel, h), other_half(rel, h)], h, extra, into_part(rel, h))

    def into_part(rel, h):
        def store(b, rows, value):
            part[SLOT[rel], h, b, rows] = value
        return store

    def cross_back(other):
        o = o_of(other)

        def step(u4, carry):
            for u in range(4):
                i = o * KX + u4 * 4 + u
                e = tile_at(POS_D + i) - POS_D
                product = lax.dot_general(cvals[e], back[ints[CROW + e // KX, e % KX]], turned, preferred_element_type=F32)
                runs_a[i + 1] = joined(POS_D + i, runs_a[i], product)
            return carry
        lax.fori_loop(0, KX // 4, step, 0)

        def one(b, carry):
            csums[o, b] = run_of(runs_a, KEY_D + o * RB + b, POS_D).astype(BF)
            return carry
        lax.fori_loop(0, RB, one, 0)

    wrows = F // N_DOM
    first = dom * wrows + here * 8

    def w_dom(n):
        return remote(wpart.at[pl.ds(doms[n] * wrows, wrows)], wquarter.at[n], ws.at[n], wr.at[n], doms[n], dev)

    def w_plane(n):
        dx, dy = plane[n]
        there = ((x + dx) % NX) * NY + (yh + dy) % NY
        return remote(wquarter.at[3, pl.ds(there * 8, 8)], wplane.at[n], ws.at[3 + n], wr.at[3 + n],
                      dom, pdev(dx, dy))

    def w_line(n):
        return remote(wplane.at[7], wline.at[z], ws.at[10 + n], wr.at[10 + n], dom, zdev(RELS[1 + n]))

    def w_plane_back(n):
        dx, dy = plane[n]
        rows = pl.ds(first, 8)
        return remote(wg.at[rows], wg.at[rows], ws.at[17 + n], wr.at[17 + n], dom, pdev(dx, dy))

    def w_dom_back(n):
        rows = pl.ds(dom * wrows, wrows)
        return remote(wg.at[rows], wg.at[rows], ws.at[24 + n], wr.at[24 + n], doms[n], dev)

    def w_step(step):
        if step == 0:
            wpart[...] = jnp.zeros_like(wpart)

            def add(r, carry):
                wpart[...] += lax.dot_general(agg[r], grad[r], turned, preferred_element_type=F32)
                return carry
            lax.fori_loop(0, RB, add, 0)
            for n in range(3):
                go(w_dom(n))
        if step == 1:
            for n in range(3):
                w_dom(n).wait_recv()
            wquarter[3] = (wpart[pl.ds(dom * wrows, wrows)] + wquarter[0]) + (wquarter[1] + wquarter[2])
            for n in range(7):
                go(w_plane(n))
        if step == 2:
            for n in range(7):
                w_plane(n).wait_recv()
            total = wquarter[3, pl.ds(here * 8, 8)]
            for n in range(7):
                total = total + wplane[n]
            wplane[7] = total
            wline[z] = total
            for n in range(7):
                go(w_line(n))
        if step == 3:
            for n in range(7):
                w_line(n).wait_recv()
            total = wline[0]
            for n in range(1, NZ):
                total = total + wline[n]
            wg[pl.ds(first, 8)] = total * W_SCALE
            for n in range(7):
                go(w_plane_back(n))
        if step == 4:
            for n in range(7):
                w_plane_back(n).wait_recv()
            for n in range(3):
                go(w_dom_back(n))
        if step == 5:
            for n in range(3):
                w_dom_back(n).wait_recv()

    def bd(n, h=0):
        if n == 0:
            return remote(csums.at[o_of(sf)], pair, bds.at[0], bdr.at[0], sib, dev)
        if n == 1:
            return remote(csums.at[o_of(sib)], near, bds.at[1], bdr.at[1], sib, dev)
        return remote(far_in.at[:, :, halves[h]], far_got.at[:, :, halves[h]], bds.at[2 + h], bdr.at[2 + h],
                      far, dev)

    def sum_far(h):
        bycopy(0, h).wait_recv()

        def store(b, rows, value):
            far_in[b, rows, halves[h]] = value
        combine([(ybuf.at[0, h], NZ, yo)], h,
                [pair.at[:, :, halves[h]], csums.at[o_of(far), :, :, halves[h]]], store)

    turns = [(4, 0), (4, 1)] + [(s * j, h if s > 0 else 1 - h)
                                for j in (3, 2, 1) for h in (0, 1) for s in (1, -1)] + [(0, 0), (0, 1)]
    n_turns = len(turns)
    queue = turns[:6] + [(0, 0), (0, 1)] + turns[6:14]
    filled = set()
    sent = {"x": 0, "y": 0}

    def xgo(upto):
        while sent["x"] < min(upto, n_turns):
            rel, h = queue[sent["x"]]
            if rel not in filled:
                filled.add(rel)
                fill(rel)
            xsend(rel, h)
            sent["x"] += 1

    def ygo(upto):
        while sent["y"] < min(upto, n_turns):
            ysend(*queue[sent["y"]])
            sent["y"] += 1

    def finish(n):
        rel, h = turns[n]
        if rel == 4:
            sum_chunk(4, h, [])
            go(rcopy(4, 3, 0) if h == 0 else lcopy(4, 3, 1))
        elif rel > 0:
            extra = []
            if rel < 3 or h == 0:
                rcopy(4, rel, h).wait_recv()
                extra = [rin.at[rel, h]]
            sum_chunk(rel, h, extra)
            go(rcopy(rel, rel - 1, h))
        elif rel < 0:
            extra = []
            if rel > -3 or h == 1:
                lcopy(4, -rel, h).wait_recv()
                extra = [lin.at[-rel, h]]
            sum_chunk(rel, h, extra)
            go(lcopy(rel, -rel - 1, h))
        else:
            rcopy(4, 0, h).wait_recv()
            lcopy(4, 0, h).wait_recv()
            cols = pl.ds(h * HW, HW)

            def store(b, rows, value):
                out[b, rows, cols] = value
            combine([own_half(0, h)], h, [rin.at[0, h], lin.at[0, h], near.at[:, :, cols], far_got.at[:, :, cols]], store)

    xgo(6)
    to_act = load(act, act_hbm)
    w_step(0)
    ygo(1)
    cross_back(sf)
    go(bd(0))
    ygo(2)
    cross_back(far)
    xgo(8)
    ygo(3)
    for n in range(n_turns):
        lead = 4 if n < 3 else 5 if n < 5 else 6
        xgo(n + lead + 3)
        ygo(n + lead)
        if n == 8:
            bd(0).wait_recv()
        if n in (8, 9):
            sum_far(n - 8)
        if n in (10, 11):
            go(bd(2, n - 10))
        if n == n_turns - 2:
            bd(1).wait_recv()
        if n >= n_turns - 2:
            bd(2, n - n_turns + 2).wait_recv()
        finish(n)
        if n == 1:
            cross_back(sib)
            go(bd(1))
        if n in (2, 4, 6, 8):
            w_step(n // 2)
    w_step(5)
    for copy in live:
        copy.wait_send()
    to_act.wait()


def run(ints, features, intra_vals, cross_vals, weight, cotangent):
    vm = pl.BlockSpec(memory_space=pltpu.VMEM)
    sm = pl.BlockSpec(memory_space=pltpu.SMEM)
    hbm = pl.BlockSpec(memory_space=pl.ANY)
    dma = pltpu.SemaphoreType.DMA
    block = (RB, BLK, F)
    half = (RB, BLK, HW)
    V = pltpu.VMEM
    return pl.pallas_call(
        kernel,
        out_shape=(
            jax.ShapeDtypeStruct(block, BF),
            jax.ShapeDtypeStruct(block, BF),
            jax.ShapeDtypeStruct((F, F), F32),
        ),
        in_specs=[sm, vm, hbm, hbm, hbm, vm, hbm],
        out_specs=(hbm, vm, vm),
        scratch_shapes=[V(block, BF)] + [V(half, BF)] * 16 + [
            V((NZ, 2, NY, NX, BLK, HW), BF),
            V((NZ, 2, NX, BLK, HW), BF),
            V((2, NX, NY, NZ, BLK, HW), BF),
            V(block, BF), V(half, BF), V(half, BF), V(block, BF),
            V((KIN, BLK, BLK), BF), V((NCROSS, BLK, BLK), BF),
            V(block, BF), V(block, BF), V(block, BF), V(block, BF), V(block, BF),
            V((NCROSS + 1, BLK, F), F32), V((KIN + 1, BLK, F), F32),
            V((N_POS, 256), I32), V((4, 8, 256), I32), pltpu.SMEM((4, 8, 256), I32),
            V((NZ + 1, 8, 128), I32), pltpu.SMEM((NZ + 1, 8, 128), I32),
            V((NZ, 2, NX, NY, BLK, HW), BF),
            V((NZ, 2, NX, BLK, HW), BF),
            V((NZ, 2) + half, BF),
            V((4, 2) + half, BF), V((4, 2) + half, BF),
            V((N_DOM - 1,) + block, BF),
            V(block, BF), V(block, BF), V(block, BF), V(block, BF),
            V((F, F), F32), V((4, F // N_DOM, F), F32), V((8, 8, F), F32), V((NZ, 8, F), F32),
            dma((9,)), dma((NZ + 1,)), dma((NZ + 1,)),
            dma((2 * NZ,)), dma((2 * NZ,)),
            dma((NZ, 2, 2, 4)), dma((NZ, 2, 2, 4)),
            dma((NZ, 2)), dma((NZ, 2)),
            dma((NZ, 2, 2)),
            dma((5,)), dma((5,)),
            dma((NZ, 2, 4)), dma((NZ, 2, 4)), dma((NZ, 2)),
            dma((NZ, 2)), dma((NZ, 2)),
            dma((4, 2)), dma((4, 2)), dma((4, 2)), dma((4, 2)),
            dma((4,)), dma((4,)),
            dma((27,)), dma((27,)),
        ],
        compiler_params=pltpu.CompilerParams(
            collective_id=0, has_side_effects=True, vmem_limit_bytes=60 << 20),
        name="graph_layer",
    )(ints, ints, features, intra_vals, cross_vals, weight, cotangent)


def deliver_kernel(*refs):
    srcs, dsts, sems = refs[:3], refs[3:6], refs[6]
    copies = [pltpu.make_async_copy(a, b, sems.at[n]) for n, (a, b) in enumerate(zip(srcs, dsts))]
    for copy in copies:
        copy.start()
    for copy in copies:
        copy.wait()


def deliver(*arrays):
    vm = pl.BlockSpec(memory_space=pltpu.VMEM)
    hbm = pl.BlockSpec(memory_space=pl.ANY)
    return pl.pallas_call(
        deliver_kernel,
        out_shape=tuple(jax.ShapeDtypeStruct(a.shape, a.dtype) for a in arrays),
        in_specs=[vm] * 3,
        out_specs=(hbm,) * 3,
        scratch_shapes=[pltpu.SemaphoreType.DMA((3,))],
        name="deliver",
    )(*arrays)


def body(features, weight, cotangent, send_list, intra_rows, intra_src, intra_count, intra_vals,
         cross_rows, cross_cols, cross_vals):
    def placed(row, values):
        flat = values.reshape((-1, values.shape[-1]))
        return jnp.pad(flat, ((row, 16 - row - flat.shape[0]), (0, 128 - flat.shape[1])))

    ints = (placed(SEND, send_list.reshape(1, -1)) + placed(IROW, intra_rows) + placed(ISRC, intra_src)
            + placed(ICOUNT, intra_count) + placed(CROW, cross_rows) + placed(CCOL, cross_cols))
    act, input_grad, weight_grad = run(
        ints, features.reshape(RB, BLK, F), intra_vals[0, 0],
        cross_vals.reshape(NCROSS, BLK, BLK), weight, cotangent.reshape(RB, BLK, F))
    act, input_grad, weight_grad = deliver(act, input_grad, weight_grad)
    return act.reshape(RB * BLK, F), input_grad.reshape(RB * BLK, F), weight_grad


def solution(mesh):
    placed = (
        P(("dom", "dev"), None),
        P(),
        P(("dom", "dev"), None),
        P("dom", "dev", None, None),
        P("dom", "dev", None),
        P("dom", "dev", None),
        P("dom", "dev"),
        P("dom", "dev", None, None, None),
        P("dom", "dev", None, None),
        P("dom", "dev", None, None),
        P("dom", "dev", None, None, None, None),
    )
    return jax.shard_map(
        body,
        mesh=mesh,
        in_specs=placed,
        out_specs=(P(("dom", "dev"), None), P(("dom", "dev"), None), P()),
        check_vma=False,
    )
```
